128 devices in a mesh: replica: 8 (over y, core), group: 16 (over x, z).
Axes of the slice: x: 4, y: 4, z: 4, core: 2. Of those that a mesh axis runs over, the one named last changes fastest.
Arguments:
- layer_input: bfloat16 [98304, 4096], P(('replica', 'group')), may hold values from -50 to 50
- up_cotangent: bfloat16 [98304, 1792], P(('replica', 'group')), may hold values from -1.5 to 1.5
- attn_values: bfloat16 [98304, 512], P(('replica', 'group')), may hold values from -6 to 6
- resid_cotangent: bfloat16 [98304, 4096], P(('replica', 'group')), may hold values from -12.5 to 12.5
- feedback: float32 [8, 4096, 2304], P('replica', 'group'), may hold values from -6 to 6
- start_seed: int32 [1], replicated, may hold values from 0 to 999999
Outputs:
- update: bfloat16 [4096, 2304], P(None, 'replica')
- new_feedback: float32 [8, 4096, 2304], P('replica', 'group')
The draws below stay inside these ranges and needn't reach their ends.
All inputs are finite; a program needn't handle non-finite values.
Results may differ from the reference program's by a relative error of at most 0.001.
Values may be sent and summed in bfloat16 or wider, within the bound.
A program may use at most 256 MiB of HBM per device.

```python
import jax
import jax.numpy as jnp
from jax import lax

D = 4096
FF = 1792
HD = 512
RANK = 32
TOK_DEV = 768
TOKENS = 98304
N_REPLICA = 8
N_GROUP = 16


def scaled_columns(key, scale):
    ramp = 10.0 ** (jnp.arange(D, dtype=jnp.float32) / D)
    values = jax.random.normal(key, (TOKENS, D), jnp.float32)
    values = jnp.clip(values, -5.0, 5.0)
    return (values * ramp[None, :] * scale).astype(jnp.bfloat16)


def draw_layer_input(key, part):
    key = jax.random.fold_in(key, 11)
    return scaled_columns(key, 1.0)


def draw_resid_cotangent(key, part):
    key = jax.random.fold_in(key, 23)
    return scaled_columns(key, 0.25)


def levels(stream_key, shape, pieces, least, high):
    factor_of, own = 1.0, jax.random.fold_in(stream_key, 6)
    for position, parts in pieces:
        draws = jnp.exp(jax.random.uniform(jax.random.fold_in(own, position), (parts,), jnp.float32, least / len(pieces), high / len(pieces)))
        factor_of = factor_of * jnp.repeat(draws, shape[position] // parts).reshape([-1 if axis == position else 1 for axis in range(len(shape))])
    return factor_of


def bell_draw(stream_key, dims, scale, reach, split=(), kind=jnp.bfloat16):
    array = jax.random.normal(stream_key, dims, jnp.float32) * scale
    if len(split) > 0:
        array = levels(stream_key, dims, split, -0.22, 0.18) * array
    return jnp.clip(array, min=-reach, max=reach).astype(kind)


def setup_inputs(seed: int = 0) -> dict:
    key_list = jax.random.split(jax.random.key(seed), 7)
    return {
        "layer_input": draw_layer_input(jax.random.fold_in(key_list[6], 71), 0),
        "up_cotangent": bell_draw(key_list[1], (TOKENS, FF), 0.25, 1.5, ((0, 128),)),
        "attn_values": bell_draw(key_list[2], (TOKENS, HD), 1.0, 6.0, ((0, 128),)),
        "resid_cotangent": draw_resid_cotangent(jax.random.fold_in(key_list[6], 71), 0),
        "feedback": bell_draw(key_list[4], (N_REPLICA, D, FF + HD), 1.0, 6.0, ((0, 8), (1, 16)), jnp.float32),
        "start_seed": jax.random.randint(key_list[5], (1,), 0, 1000000).astype(jnp.int32),
    }


def make_factor(start_seed, count, layer):
    positions = jnp.arange(count, dtype=jnp.int32)[:, None]
    columns = jnp.arange(RANK, dtype=jnp.int32)[None, :]
    base = start_seed[0].astype(jnp.int32) % 65521
    mixed = (base * 31 + positions * 977 + columns * 7919 + layer * 4099 + 12345) % 65521
    folded = mixed % 256 * (mixed // 256) % 65521
    final = (folded * 181 + mixed) % 65521
    return (final.astype(jnp.float32) / 65521.0 - 0.5) * 3.4

def highest(left, right):
    return jnp.dot(left, right, precision=lax.Precision.HIGHEST)

def orthonormal(factor):
    gram = highest(factor.T, factor)
    lower = jnp.linalg.cholesky(gram)
    return jax.scipy.linalg.solve_triangular(lower, factor.T, lower=True).T

def reference(layer_input, up_cotangent, attn_values, resid_cotangent, feedback, start_seed):
    block = TOK_DEV * N_GROUP
    matrices = []
    for member in range(N_REPLICA):
        rows = slice(member * block, (member + 1) * block)
        first = jnp.dot(layer_input[rows].T.astype(jnp.float32), up_cotangent[rows].astype(jnp.float32), preferred_element_type=jnp.float32)
        second = jnp.dot(resid_cotangent[rows].T.astype(jnp.float32), attn_values[rows].astype(jnp.float32), preferred_element_type=jnp.float32)
        matrices.append(jnp.concatenate([first, second], axis=1) / N_GROUP + feedback[member])
    factor_left = make_factor(start_seed, FF, 0)
    factor_right = make_factor(start_seed, HD, 1)
    mean_left = sum((highest(m[:, :FF], factor_left) for m in matrices)) / N_REPLICA
    mean_right = sum((highest(m[:, FF:], factor_right) for m in matrices)) / N_REPLICA
    basis_left = orthonormal(mean_left)
    basis_right = orthonormal(mean_right)
    back_left = sum((highest(m[:, :FF].T, basis_left) for m in matrices)) / N_REPLICA
    back_right = sum((highest(m[:, FF:].T, basis_right) for m in matrices)) / N_REPLICA
    approx = jnp.concatenate([highest(basis_left, back_left.T), highest(basis_right, back_right.T)], axis=1)
    new_feedback = jnp.stack([m - approx for m in matrices])
    return (approx.astype(jnp.bfloat16), new_feedback)
```

```python
import jax
import jax.numpy as jnp
from jax import lax
from jax.experimental import pallas as pl
from jax.experimental.pallas import tpu as pltpu
from jax.sharding import PartitionSpec as P

RANK = 32
TOK = 768
D = 4096
FF = 1792
HD = 512
W = FF + HD
HALF = W // 2
ROWS = 256
SIDE = 4
GROUP = 16
REP = 8
BLEN = 2048
LEVELS = 32700.0
ORDER = (2, 1, 3, 0)
MESH = pl.DeviceIdType.MESH
F32 = jnp.float32
BF16 = jnp.bfloat16
OPP_A, OPP_B, PURE_B, PURE_A, DEP_A, DEP_B = range(6)
RIGHTWARD = (True, False, True, False, True, False)


def make_factor_t(start_seed, count, layer):
    positions = jnp.arange(count, dtype=jnp.int32)[None, :]
    columns = jnp.arange(RANK, dtype=jnp.int32)[:, None]
    base = start_seed[0] % 65521
    mixed = (base * 31 + positions * 977 + columns * 7919 + layer * 4099 + 12345) % 65521
    folded = mixed % 256 * (mixed // 256) % 65521
    final = (folded * 181 + mixed) % 65521
    return (final.astype(F32) / 65521.0 - 0.5) * 3.4


def split3(v):
    hi = v.astype(BF16)
    rest = v - hi.astype(F32)
    mid = rest.astype(BF16)
    low = (rest - mid.astype(F32)).astype(BF16)
    return jnp.concatenate([hi, mid, low], axis=0)


def split2(v):
    hi = v.astype(BF16)
    return hi, (v - hi.astype(F32)).astype(BF16)


def fold3(v):
    return (v[64:96] + v[32:64]) + v[0:32]


def dot_nn(a, b):
    return lax.dot_general(a, b, (((1,), (0,)), ((), ())), preferred_element_type=F32)


def dot_nt(a, b):
    return lax.dot_general(a, b, (((1,), (1,)), ((), ())), preferred_element_type=F32)


def dot_nn_full(a, b):
    return lax.dot_general(
        a, b, (((1,), (0,)), ((), ())), precision=lax.Precision.HIGHEST, preferred_element_type=F32
    )


def dot_nt_full(a, b):
    return lax.dot_general(
        a, b, (((1,), (1,)), ((), ())), precision=lax.Precision.HIGHEST, preferred_element_type=F32
    )


def peak8(v):
    return jnp.max(jnp.abs(v).reshape(v.shape[0] // 8, 8, v.shape[1]), axis=0)


def at(start, size, step):
    return pl.ds(pl.multiple_of(start, step), size)


def inverse_factor(gram):
    row = lax.broadcasted_iota(jnp.int32, (RANK, RANK), 0)
    lane = lax.broadcasted_iota(jnp.int32, (RANK, RANK), 1)
    eye = jnp.where(row == lane, 1.0, 0.0).astype(F32)

    def step(j, state):
        out = []
        for a, b in state:
            col = jnp.sum(jnp.where(lane == j, a, 0.0), axis=1, keepdims=True)
            a_row = jnp.sum(jnp.where(row == j, a, 0.0), axis=0, keepdims=True)
            b_row = jnp.sum(jnp.where(row == j, b, 0.0), axis=0, keepdims=True)
            pivot = jnp.sum(jnp.where((row == j) & (lane == j), a, 0.0), axis=(0, 1), keepdims=True)
            factor = jnp.where(row[:, :1] > j, col / pivot, 0.0)
            out.append((a - factor * a_row, b - factor * b_row))
        return tuple(out)

    state = lax.fori_loop(0, RANK, step, tuple((g, eye) for g in gram))
    result = []
    for a, b in state:
        diag = jnp.sum(jnp.where(row == lane, a, 0.0), axis=1, keepdims=True)
        result.append(b * (1.0 / jnp.sqrt(diag)))
    return result


def kernel(
    x_hbm, u_hbm, a_hbm, g_hbm, fb_hbm, qt_ref,
    new_hbm, upd_hbm,
    xs, gs, ut, ustg, tmp, pdep, pown, tx, rx, fb,
    pt, prx, psum, prx2, psl, pg, pall,
    bt, brx, bsum, brx2, bsl, bg, ball, bk4, uout,
    load_x, load_g, load_u, load_fb, out_sem,
    tx_sem, rx_sem, small_tx, small_rx,
):
    group = lax.axis_index("group")
    rep = lax.axis_index("replica")
    gx = group // SIDE
    gz = group % SIDE

    def member(dx, dz):
        return (gx + dx) % SIDE * SIDE + (gz + dz) % SIDE

    ucopies = []
    for t in range(9):
        src = u_hbm.at[:, pl.ds(256 * t, 256)] if t < 7 else a_hbm.at[:, pl.ds(256 * (t - 7), 256)]
        ucopies.append(pltpu.make_async_copy(src, ustg.at[t % 2], load_u.at[t % 2]))
    ucopies[0].start()
    ucopies[1].start()
    steps = [(df, ds) for ds in ORDER for df in ORDER]
    for i, (df, ds) in enumerate(steps):
        low = at(ROWS * member(df, ds), 128, 128)
        high = at(ROWS * member(ds, df) + 128, 128, 128)
        pltpu.make_async_copy(x_hbm.at[:, low], xs.at[i, :, pl.ds(0, 128)], load_x.at[i]).start()
        pltpu.make_async_copy(x_hbm.at[:, high], xs.at[i, :, pl.ds(128, 128)], load_x.at[i]).start()
        pltpu.make_async_copy(g_hbm.at[:, low], gs.at[i, :, pl.ds(0, 128)], load_g.at[i]).start()
        pltpu.make_async_copy(g_hbm.at[:, high], gs.at[i, :, pl.ds(128, 128)], load_g.at[i]).start()
    pltpu.make_async_copy(fb_hbm, fb, load_fb).start()

    loaded = set()

    def wait_step(i):
        if i in loaded:
            return
        loaded.add(i)
        pltpu.make_async_copy(xs.at[i], xs.at[i], load_x.at[i]).wait()
        pltpu.make_async_copy(gs.at[i], gs.at[i], load_g.at[i]).wait()

    barrier = pltpu.get_barrier_semaphore()

    @pl.loop(1, GROUP)
    def _(d):
        pl.semaphore_signal(barrier, inc=1, device_id={"group": (group + d) % GROUP}, device_id_type=MESH)

    @pl.loop(1, REP)
    def _(d):
        pl.semaphore_signal(barrier, inc=1, device_id={"replica": (rep + d) % REP}, device_id_type=MESH)

    for t in range(9):
        ucopies[t].wait()
        ut[256 * t : 256 * t + 256, :] = ustg[t % 2].T
        if t + 2 < 9:
            ucopies[t + 2].start()

    def matmul(i, first, dst, base):
        def tile(source, size, start, to):
            r = dot_nn(ut[at(start, size, 64), :], source[i])
            dst[at(to, size, 64), :] = r
            return peak8(r)

        zero = jnp.zeros((8, ROWS), F32)
        if first:
            return lax.fori_loop(
                0, 3, lambda t, m: jnp.maximum(m, tile(xs, 384, t * 384, base + t * 384)), zero
            )
        m = lax.fori_loop(
            0, 2, lambda t, m: jnp.maximum(m, tile(xs, 320, HALF + t * 320, base + t * 320)), zero
        )
        return lax.fori_loop(
            0, 2, lambda t, m: jnp.maximum(m, tile(gs, 256, FF + t * 256, base + 640 + t * 256)), m
        )

    def quantise(src, base, m, slot):
        peak = jnp.maximum(jnp.max(m, axis=0, keepdims=True), 1e-30)
        power = jnp.ceil(jnp.log2(peak))
        scale = jnp.exp2(-power) * LEVELS

        @pl.loop(0, HALF // 64)
        def _(t):
            v = src[at(base + t * 64, 64, 64), :] * scale
            tx[slot, at(t * 64, 64, 64), :] = jnp.round(v).astype(jnp.int32).astype(jnp.int16)

        tx[slot, HALF : HALF + 16, :] = jnp.broadcast_to(power, (16, ROWS)).astype(jnp.int32).astype(jnp.int16)

    def copy_of(slot, mid, kind, stage, h):
        lanes = pl.ds(128 * h, 128)
        along_x = (h == 0) == (stage == 0)
        step = 1 if RIGHTWARD[kind] else SIDE - 1
        peer = member(step, 0) if along_x else member(0, step)
        return pltpu.make_async_remote_copy(
            src_ref=tx.at[slot, :, lanes],
            dst_ref=rx.at[mid, :, lanes],
            send_sem=tx_sem.at[mid, h],
            recv_sem=rx_sem.at[mid, h],
            device_id={"group": peer},
            device_id_type=MESH,
        )

    def slot_of(mid):
        chunk, kind = divmod(mid, 6)
        if chunk == 4:
            return 8 + kind
        return kind + (6 if chunk % 2 and kind < 2 else 0)

    def copies(mid):
        chunk, kind = divmod(mid, 6)
        return [copy_of(slot_of(mid), mid, kind, chunk // 4, h) for h in range(2)]

    pending = {}

    def send(mid, src, base, m):
        slot = slot_of(mid)
        if slot in pending:
            for c in copies(pending[slot]):
                c.wait_send()
        quantise(src, base, m, slot)
        for c in copies(mid):
            c.start()
        pending[slot] = mid

    def combine(acc, base, mids):
        for mid in mids:
            for c in copies(mid):
                c.wait_recv()
        scales = [
            jnp.exp2(rx[mid, HALF : HALF + 16, :].astype(jnp.int32).astype(F32)[:8]) * (1.0 / LEVELS)
            for mid in mids
        ]

        def tile(t, m):
            v = acc[at(base + t * 64, 64, 64), :].reshape(8, 8, ROWS)
            for mid, scale in zip(mids, scales):
                got = rx[mid, at(t * 64, 64, 64), :].astype(jnp.int32).astype(F32).reshape(8, 8, ROWS)
                v = v + got * scale[None]
            acc[at(base + t * 64, 64, 64), :] = v.reshape(64, ROWS)
            return jnp.maximum(m, jnp.max(jnp.abs(v), axis=0))

        return lax.fori_loop(0, HALF // 64, tile, jnp.zeros((8, ROWS), F32))

    def opposite(k):
        wait_step(4 * k)
        m = matmul(4 * k, True, tmp, 0)
        send(6 * k + OPP_A, tmp, 0, m)
        m = matmul(4 * k, False, tmp, 0)
        send(6 * k + OPP_B, tmp, 0, m)

    def pure(k):
        wait_step(4 * k + 1)
        m = matmul(4 * k + 1, False, tmp, 0)
        send(6 * k + PURE_B, tmp, 0, m)
        wait_step(4 * k + 2)
        m = matmul(4 * k + 2, True, tmp, 0)
        send(6 * k + PURE_A, tmp, 0, m)
        matmul(4 * k + 1, True, pdep, 0)
        matmul(4 * k + 2, False, pdep, HALF)

    def own(k):
        wait_step(4 * k + 3)
        matmul(4 * k + 3, True, pown, 0)
        matmul(4 * k + 3, False, pown, HALF)

    def dependent(k):
        m = combine(pdep, 0, [6 * k + OPP_A])
        send(6 * k + DEP_A, pdep, 0, m)
        m = combine(pdep, HALF, [6 * k + OPP_B])
        send(6 * k + DEP_B, pdep, HALF, m)

    def complete(k):
        more_a = {0: [], 1: [24 + OPP_A], 2: [], 3: [24 + DEP_A, 24 + PURE_A]}[k]
        more_b = {0: [], 1: [], 2: [24 + OPP_B], 3: [24 + PURE_B, 24 + DEP_B]}[k]
        kind_a = {0: OPP_A, 1: DEP_A, 2: PURE_A}.get(k)
        kind_b = {0: OPP_B, 1: PURE_B, 2: DEP_B}.get(k)
        m = combine(pown, 0, [6 * k + DEP_A, 6 * k + PURE_A] + more_a)
        if k < 3:
            send(24 + kind_a, pown, 0, m)
        m = combine(pown, HALF, [6 * k + PURE_B, 6 * k + DEP_B] + more_b)
        if k < 3:
            send(24 + kind_b, pown, HALF, m)

    def rep_scatter_copy(src, dst, d, which):
        peer = (rep + d) % REP
        return pltpu.make_async_remote_copy(
            src_ref=src.at[at(peer * 8, 8, 8), :],
            dst_ref=dst.at[d - 1],
            send_sem=small_tx.at[which],
            recv_sem=small_rx.at[which],
            device_id={"replica": peer},
            device_id_type=MESH,
        )

    def rep_scatter(src, dst, which):
        @pl.loop(1, REP)
        def _(d):
            rep_scatter_copy(src, dst, d, which).start()

    def group_scatter(src, dst, which):
        width = src.shape[1] // GROUP

        @pl.loop(1, GROUP)
        def _(d):
            peer = (group + d) % GROUP
            pltpu.make_async_remote_copy(
                src_ref=src.at[:, at(peer * width, width, 128)],
                dst_ref=dst.at[d - 1],
                send_sem=small_tx.at[which],
                recv_sem=small_rx.at[which],
                device_id={"group": peer},
                device_id_type=MESH,
            ).start()

    def group_gather(src, dst, which):
        width = src.shape[1]
        mine = at(group * width, width, 128)
        dst[:, mine] = src[...]

        @pl.loop(1, GROUP)
        def _(d):
            pltpu.make_async_remote_copy(
                src_ref=src,
                dst_ref=dst.at[:, mine],
                send_sem=small_tx.at[which],
                recv_sem=small_rx.at[which],
                device_id={"group": (group + d) % GROUP},
                device_id_type=MESH,
            ).start()

    def rep_gather(src, dst, which):
        mine = at(rep * 8, 8, 8)
        dst[mine, :] = src[...]

        @pl.loop(1, REP)
        def _(d):
            pltpu.make_async_remote_copy(
                src_ref=src,
                dst_ref=dst.at[mine, :],
                send_sem=small_tx.at[which],
                recv_sem=small_rx.at[which],
                device_id={"replica": (rep + d) % REP},
                device_id_type=MESH,
            ).start()

    def await_bytes(ref, sem):
        pltpu.make_async_copy(ref, ref, sem).wait()

    def after_rep_scatter(src, dst, total, which):
        await_bytes(dst, small_rx.at[which])
        value = src[at(rep * 8, 8, 8), :]
        for d in range(REP - 1):
            value = value + dst[d]
        total[...] = value

    def after_group_scatter(src, dst, total, which):
        await_bytes(dst, small_rx.at[which])
        width = src.shape[1] // GROUP
        value = src[:, at(group * width, width, 128)]
        for d in range(GROUP - 1):
            value = value + dst[d]
        total[...] = value

    def after_group_gather(dst, width, which):
        await_bytes(dst.at[:, pl.ds(0, 15 * width)], small_rx.at[which])

    def after_rep_gather(dst, which):
        await_bytes(dst.at[pl.ds(0, 56), :], small_rx.at[which])

    def place(i):
        k, j = i // 4, i % 4
        df = jnp.where(j == 0, 2, jnp.where(j == 1, 1, jnp.where(j == 2, 3, 0)))
        ds = jnp.where(k == 0, 2, jnp.where(k == 1, 1, jnp.where(k == 2, 3, 0)))
        return (
            at(ROWS * member(df, ds), 128, 128),
            at(ROWS * member(ds, df) + 128, 128, 128),
        )

    def project():
        q_l, q_r = split3(qt_ref[:, :FF]), split3(qt_ref[:, FF:])
        w_l = split3(fold3(dot_nn(q_l, ut[:FF, :])))
        w_r = split3(fold3(dot_nn(q_r, ut[FF:, :])))

        @pl.loop(0, GROUP)
        def _(i):
            p_l = fold3(dot_nn(w_l, xs[i])) * (1.0 / 128)
            p_r = fold3(dot_nn(w_r, gs[i])) * (1.0 / 128)
            low, high = place(i)
            pt[:RANK, low] = p_l[:, :128]
            pt[:RANK, high] = p_l[:, 128:]
            pt[RANK:, low] = p_r[:, :128]
            pt[RANK:, high] = p_r[:, 128:]

        mine = at(ROWS * group, ROWS, 128)
        for rows, columns, q3 in (
            (slice(0, RANK), slice(0, FF), q_l),
            (slice(RANK, 64), slice(FF, W), q_r),
        ):
            hi, low = split2(fb[:, columns])
            term = fold3(dot_nt(q3, hi)) + fold3(dot_nt(q3, low))
            pt[rows, mine] += term * (1.0 / 8)

    def back_project():
        def tile(i, state):
            y_l, y_r = state
            low, high = place(i)
            p = jnp.concatenate([pall[:, low], pall[:, high]], axis=1)
            return y_l + dot_nt(split3(p[:RANK]), xs[i]), y_r + dot_nt(split3(p[RANK:]), gs[i])

        zero = jnp.zeros((96, TOK), F32)
        y_l, y_r = lax.fori_loop(0, GROUP, tile, (zero, zero))
        y_l = split3(fold3(y_l) * (1.0 / 128))
        y_r = split3(fold3(y_r) * (1.0 / 128))
        p = pall[:, at(ROWS * group, ROWS, 128)] * (1.0 / 8)
        p_l, p_r = split3(p[:RANK]), split3(p[RANK:])

        def piece(y, p3, columns):
            hi, low = split2(fb[:, columns])
            return fold3(dot_nt(y, ut[columns, :])) + (fold3(dot_nn(p3, hi)) + fold3(dot_nn(p3, low)))

        for t in range(3):
            columns = slice(384 * t, 384 * t + 384)
            bt[:RANK, columns] = piece(y_l, p_l, columns)
        bt[RANK:, 0:640] = piece(y_l, p_l, slice(HALF, FF))
        bt[RANK:, 640:HALF] = piece(y_r, p_r, slice(FF, W))
        bt[:, HALF:] = jnp.zeros((64, BLEN - HALF), F32)

    def factors():
        gram_l = dot_nt_full(pall[:RANK, :], pall[:RANK, :])
        gram_r = dot_nt_full(pall[RANK:, :], pall[RANK:, :])
        return inverse_factor((gram_l, gram_r))

    def quad(v, last):
        hi, low = split2(v)
        return jnp.concatenate([hi, hi, low, low] if last else [hi, low, hi, low], axis=0)

    def bases(t_l, t_r, lanes):
        return jnp.concatenate(
            [
                quad(dot_nn_full(t_l, pall[:RANK, lanes]), True),
                quad(dot_nn_full(t_r, pall[RANK:, lanes]), True),
            ],
            axis=0,
        )

    def decompress(t_l, t_r):
        mine = bases(t_l, t_r, at(ROWS * group, ROWS, 128)).T
        pieces = (
            (t_l, slice(0, RANK), 0, 384, 0),
            (t_l, slice(0, RANK), 384, 768, 0),
            (t_l, slice(0, RANK), 768, 1152, 0),
            (t_l, slice(RANK, 64), 0, 640, HALF),
            (t_r, slice(RANK, 64), 640, HALF, HALF),
        )
        for t, rows, lo, hi, base in pieces:
            b4 = quad(dot_nn_full(t, ball[rows, lo:hi]), False)
            none = jnp.zeros_like(b4)
            left = base + lo < FF
            both = jnp.concatenate([b4, none] if left else [none, b4], axis=0)
            fb[:, base + lo : base + hi] -= dot_nn(mine, both)
            bk4[base + lo : base + hi, :] = both.T
        width = W // REP
        chosen = bk4[at(rep * width, width, 16), :]

        @pl.loop(0, 8)
        def _(t):
            basis = bases(t_l, t_r, at(t * 512, 512, 128)).T
            uout[at(t * 512, 512, 128), :] = dot_nt(basis, chosen).astype(BF16)

        pltpu.make_async_copy(uout, upd_hbm, out_sem.at[0]).start()

    pl.semaphore_wait(barrier, GROUP - 1 + REP - 1)

    opposite(0)
    pure(0)
    own(0)
    for i in range(4, GROUP):
        wait_step(i)
    pltpu.make_async_copy(fb_hbm, fb, load_fb).wait()
    project()
    rep_scatter(pt, prx, 0)
    opposite(1)
    dependent(0)
    pure(1)
    after_rep_scatter(pt, prx, psum, 0)
    group_scatter(psum, prx2, 1)
    complete(0)
    own(1)
    after_group_scatter(psum, prx2, psl, 1)
    group_gather(psl, pg, 2)
    opposite(2)
    dependent(1)
    after_group_gather(pg, ROWS, 2)
    rep_gather(pg, pall, 3)
    pure(2)
    complete(1)
    own(2)
    opposite(3)
    dependent(2)
    after_rep_gather(pall, 3)
    back_project()
    rep_scatter(bt, brx, 4)
    pure(3)
    complete(2)
    own(3)
    after_rep_scatter(bt, brx, bsum, 4)
    group_scatter(bsum, brx2, 5)
    dependent(3)
    t_l, t_r = factors()
    after_group_scatter(bsum, brx2, bsl, 5)
    group_gather(bsl, bg, 6)
    after_group_gather(bg, BLEN // GROUP, 6)
    rep_gather(bg, ball, 7)
    after_rep_gather(ball, 7)
    decompress(t_l, t_r)
    complete(3)

    for t in range(9):
        columns = slice(256 * t, 256 * t + 256)
        fb[:, columns] += pown[columns, :].T * (1.0 / GROUP)
    pltpu.make_async_copy(fb, new_hbm, out_sem.at[1]).start()

    for slot in pending:
        for c in copies(pending[slot]):
            c.wait_send()
    for which, ref in ((0, prx), (4, brx), (1, prx2), (5, brx2)):
        await_bytes(ref, small_tx.at[which])
    await_bytes(pg.at[:, pl.ds(0, 15 * ROWS)], small_tx.at[2])
    await_bytes(bg.at[:, pl.ds(0, 15 * (BLEN // GROUP))], small_tx.at[6])
    await_bytes(pall.at[pl.ds(0, 56), :], small_tx.at[3])
    await_bytes(ball.at[pl.ds(0, 56), :], small_tx.at[7])
    pltpu.make_async_copy(uout, upd_hbm, out_sem.at[0]).wait()
    pltpu.make_async_copy(fb, new_hbm, out_sem.at[1]).wait()


def on_device(layer_input, up_cotangent, attn_values, resid_cotangent, feedback, start_seed):
    factor = jnp.concatenate(
        [make_factor_t(start_seed, FF, 0), make_factor_t(start_seed, HD, 1)], axis=1
    )
    hbm = pl.BlockSpec(memory_space=pl.ANY)
    dma = pltpu.SemaphoreType.DMA
    new_feedback, update = pl.pallas_call(
        kernel,
        out_shape=(
            jax.ShapeDtypeStruct((ROWS, W), F32),
            jax.ShapeDtypeStruct((D, W // REP), BF16),
        ),
        in_specs=[hbm] * 5 + [pl.BlockSpec(memory_space=pltpu.VMEM)],
        out_specs=(hbm, hbm),
        scratch_shapes=[
            pltpu.VMEM((GROUP, TOK, ROWS), BF16),
            pltpu.VMEM((GROUP, TOK, ROWS), BF16),
            pltpu.VMEM((W, TOK), BF16),
            pltpu.VMEM((2, TOK, 256), BF16),
            pltpu.VMEM((HALF, ROWS), F32),
            pltpu.VMEM((W, ROWS), F32),
            pltpu.VMEM((W, ROWS), F32),
            pltpu.VMEM((14, HALF + 16, ROWS), jnp.int16),
            pltpu.VMEM((30, HALF + 16, ROWS), jnp.int16),
            pltpu.VMEM((ROWS, W), F32),
            pltpu.VMEM((64, D), F32),
            pltpu.VMEM((REP - 1, 8, D), F32),
            pltpu.VMEM((8, D), F32),
            pltpu.VMEM((GROUP - 1, 8, ROWS), F32),
            pltpu.VMEM((8, ROWS), F32),
            pltpu.VMEM((8, D), F32),
            pltpu.VMEM((64, D), F32),
            pltpu.VMEM((64, BLEN), F32),
            pltpu.VMEM((REP - 1, 8, BLEN), F32),
            pltpu.VMEM((8, BLEN), F32),
            pltpu.VMEM((GROUP - 1, 8, BLEN // GROUP), F32),
            pltpu.VMEM((8, BLEN // GROUP), F32),
            pltpu.VMEM((8, BLEN), F32),
            pltpu.VMEM((64, BLEN), F32),
            pltpu.VMEM((W, 256), BF16),
            pltpu.VMEM((D, W // REP), BF16),
            dma((GROUP,)),
            dma((GROUP,)),
            dma((2,)),
            dma,
            dma((2,)),
            dma((30, 2)),
            dma((30, 2)),
            dma((8,)),
            dma((8,)),
        ],
        compiler_params=pltpu.CompilerParams(
            collective_id=0, has_side_effects=True, vmem_limit_bytes=64 * 1024 * 1024 - 256 * 1024
        ),
        cost_estimate=pl.CostEstimate(flops=2 * TOK * D * W, bytes_accessed=21_000_000, transcendentals=0),
    )(layer_input, up_cotangent, attn_values, resid_cotangent, feedback[0], factor)
    return (update, new_feedback[None])


def solution(mesh):
    in_specs = (
        P(("replica", "group"), None),
        P(("replica", "group"), None),
        P(("replica", "group"), None),
        P(("replica", "group"), None),
        P("replica", "group", None),
        P(),
    )
    out_specs = (P(None, "replica"), P("replica", "group", None))
    return jax.shard_map(
        on_device, mesh=mesh, in_specs=in_specs, out_specs=out_specs, check_vma=False
    )
```

```python
import jax
import jax.numpy as jnp
from jax import lax
from jax.experimental import pallas as pl
from jax.experimental.pallas import tpu as pltpu
from jax.sharding import PartitionSpec as P

RANK = 32
TOK = 768
D = 4096
FF = 1792
HD = 512
W = FF + HD
HALF = W // 2
ROWS = 256
SIDE = 4
GROUP = 16
REP = 8
BLEN = 1536
LEVELS = 32700.0
ORDER = (2, 1, 3, 0)
MESH = pl.DeviceIdType.MESH
F32 = jnp.float32
BF16 = jnp.bfloat16
OPP_A, OPP_B, PURE_B, PURE_A, DEP_A, DEP_B = range(6)
RIGHTWARD = (True, False, True, False, True, False)


def modulo(v):
    r = v - jnp.floor(v * (1.0 / 65521.0)) * 65521.0
    r = jnp.where(r < 0.0, r + 65521.0, r)
    return jnp.where(r >= 65521.0, r - 65521.0, r)


def factor_t(seed, first, count, layer):
    positions = lax.broadcasted_iota(jnp.int32, (RANK, count), 1) + first
    columns = lax.broadcasted_iota(jnp.int32, (RANK, count), 0)
    base = (seed % 65521) * 31 + layer * 4099 + 12345
    mixed = modulo((base + positions * 977 + columns * 7919).astype(F32)).astype(jnp.int32)
    folded = (mixed & 255) * (mixed >> 8)
    final = modulo((folded * 181 + mixed).astype(F32))
    return (final / 65521.0 - 0.5) * 3.4


def split3(v):
    hi = v.astype(BF16)
    rest = v - hi.astype(F32)
    mid = rest.astype(BF16)
    low = (rest - mid.astype(F32)).astype(BF16)
    return jnp.concatenate([hi, mid, low], axis=0)


def split2(v):
    hi = v.astype(BF16)
    return hi, (v - hi.astype(F32)).astype(BF16)


def fold3(v):
    return (v[64:96] + v[32:64]) + v[0:32]


def dot_nn(a, b):
    return lax.dot_general(a, b, (((1,), (0,)), ((), ())), preferred_element_type=F32)


def dot_nt(a, b):
    return lax.dot_general(a, b, (((1,), (1,)), ((), ())), preferred_element_type=F32)


def dot_tn(a, b):
    return lax.dot_general(a, b, (((0,), (0,)), ((), ())), preferred_element_type=F32)


def dot_nt_full(a, b):
    return lax.dot_general(
        a, b, (((1,), (1,)), ((), ())), precision=lax.Precision.HIGHEST, preferred_element_type=F32
    )


def peak8(v):
    return jnp.max(jnp.abs(v).reshape(v.shape[0] // 8, 8, v.shape[1]), axis=0)


def at(start, size, step):
    return pl.ds(pl.multiple_of(start, step), size)


def pieces3(v):
    hi = v.astype(BF16)
    rest = v - hi.astype(F32)
    mid = rest.astype(BF16)
    return hi, mid, (rest - mid.astype(F32)).astype(BF16)


def apply_factor(t_t, v):
    hi, mid, low = pieces3(t_t)
    left = jnp.concatenate([hi, hi, hi, mid, mid, low], axis=0)
    hi, mid, low = pieces3(v)
    return dot_tn(left, jnp.concatenate([hi, mid, low, hi, mid, hi], axis=0))


def inverse_factor(gram):
    row = lax.broadcasted_iota(jnp.int32, (RANK, RANK), 0)
    lane = lax.broadcasted_iota(jnp.int32, (RANK, RANK), 1)
    eye = jnp.where(row == lane, 1.0, 0.0).astype(F32)

    def step(j, state):
        out = []
        for a, b in state:
            a_row = jnp.sum(jnp.where(row == j, a, 0.0), axis=0, keepdims=True)
            pivot = jnp.sum(jnp.where(lane[:1] == j, a_row, 0.0), axis=1, keepdims=True)
            a_col = jnp.sum(jnp.where(lane == j, a, 0.0), axis=1, keepdims=True)
            b_col = jnp.sum(jnp.where(lane == j, b, 0.0), axis=1, keepdims=True)
            factor = jnp.where(lane[:1] > j, a_row / pivot, 0.0)
            out.append((a - a_col * factor, b - b_col * factor))
        return tuple(out)

    state = lax.fori_loop(0, RANK, step, tuple((g, eye) for g in gram))
    result = []
    for a, b in state:
        diag = jnp.sum(jnp.where(row == lane, a, 0.0), axis=0, keepdims=True)
        result.append(b * (1.0 / jnp.sqrt(diag)))
    return result


def kernel(
    x_hbm, u_hbm, a_hbm, g_hbm, fb_hbm, seed_ref,
    new_hbm, upd_hbm,
    xs, gs, ut, ustg, tmp, pdep, pown, tx, rx, fb, q3,
    pt, pc, ps, py, pz, px, pall,
    bt, bc, bs, by, bz, bx, ball, bk4, uout,
    load_x, load_g, load_u, load_fb, out_sem,
    tx_sem, rx_sem, small_tx, small_rx,
):
    group = lax.axis_index("group")
    rep = lax.axis_index("replica")
    gx = group // SIDE
    gz = group % SIDE
    ry = rep // 2
    rc = rep % 2

    def member(dx, dz):
        return (gx + dx) % SIDE * SIDE + (gz + dz) % SIDE

    def replica(dy, dc):
        return (ry + dy) % SIDE * 2 + (rc + dc) % 2

    def load_step(k, j):
        df, ds = ORDER[j], ORDER[k]
        low = at(ROWS * member(df, ds), 128, 128)
        high = at(ROWS * member(ds, df) + 128, 128, 128)
        for src, dst, sem in ((x_hbm, xs, load_x), (g_hbm, gs, load_g)):
            for part, lanes in enumerate((low, high)):
                pltpu.make_async_copy(
                    src.at[:, lanes], dst.at[k, :, pl.ds(256 * j + 128 * part, 128)], sem.at[4 * k + j]
                ).start()

    load_a = pltpu.make_async_copy(u_hbm.at[:, pl.ds(0, HALF)], ustg, load_u.at[0])
    load_b = pltpu.make_async_copy(
        u_hbm.at[:, pl.ds(HALF, FF - HALF)], ustg.at[:, pl.ds(0, FF - HALF)], load_u.at[1]
    )
    load_c = pltpu.make_async_copy(a_hbm, ustg.at[:, pl.ds(FF - HALF, HD)], load_u.at[2])
    load_a.start()
    for k in range(SIDE):
        for j in range(SIDE):
            load_step(k, j)
    pltpu.make_async_copy(fb_hbm, fb, load_fb).start()
    loaded = set()

    def wait_step(k, j):
        if (k, j) in loaded:
            return
        loaded.add((k, j))
        for ref, sem in ((xs, load_x), (gs, load_g)):
            part = ref.at[k, :, pl.ds(256 * j, 256)]
            pltpu.make_async_copy(part, part, sem.at[4 * k + j]).wait()

    barrier = pltpu.get_barrier_semaphore()

    def greet(dy, dc, dx, dz):
        pl.semaphore_signal(
            barrier,
            inc=1,
            device_id={"replica": replica(dy, dc), "group": member(dx, dz)},
            device_id_type=MESH,
        )

    greet(0, 1, 0, 0)
    for d in range(1, SIDE):
        greet(d, 0, 0, 0)
        greet(1, 0, 0, d)
        greet(SIDE - 1, 0, 0, d)
        greet(0, 0, d, 0)
    greet(0, 0, 0, 1)
    greet(0, 0, 0, SIDE - 1)

    def transpose_u(base, sizes):
        start = 0
        for size in sizes:
            ut[base + start : base + start + size, :] = ustg[:, start : start + size].T
            start += size

    A_TILES = ((0, HALF, xs),)
    B_TILES = ((HALF, FF - HALF, xs), (FF, HD, gs))

    def products(k, lanes, tiles):
        row = 0
        for start, size, source in tiles:
            yield row, size, dot_nn(ut[start : start + size, :], source[k, :, lanes])
            row += size

    def matmul(k, j, tiles, dst, base):
        peak = jnp.zeros((8, ROWS), F32)
        for row, size, value in products(k, slice(256 * j, 256 * j + 256), tiles):
            dst[base + row : base + row + size, :] = value
            peak = jnp.maximum(peak, peak8(value))
        return peak

    def matmul_pair(k, tiles, dst_1, base_1, dst_2, base_2):
        peak = jnp.zeros((8, 2 * ROWS), F32)
        for row, size, value in products(k, slice(256, 768), tiles):
            dst_1[base_1 + row : base_1 + row + size, :] = value[:, :ROWS]
            dst_2[base_2 + row : base_2 + row + size, :] = value[:, ROWS:]
            peak = jnp.maximum(peak, peak8(value))
        return peak[:, :ROWS], peak[:, ROWS:]

    def quantise(src, base, m, slot):
        peak = jnp.maximum(jnp.max(m, axis=0, keepdims=True), 1e-30)
        power = jnp.ceil(jnp.log2(peak))
        scale = jnp.exp2(-power) * LEVELS

        @pl.loop(0, HALF // 64)
        def _(t):
            v = src[at(base + t * 64, 64, 64), :] * scale
            tx[slot, at(t * 64, 64, 64), :] = jnp.round(v).astype(jnp.int32).astype(jnp.int16)

        tx[slot, HALF : HALF + 16, :] = jnp.broadcast_to(power, (16, ROWS)).astype(jnp.int32).astype(jnp.int16)

    def copy_of(slot, mid, kind, stage, h):
        lanes = pl.ds(128 * h, 128)
        along_x = (h == 0) == (stage == 0)
        step = 1 if RIGHTWARD[kind] else SIDE - 1
        peer = member(step, 0) if along_x else member(0, step)
        return pltpu.make_async_remote_copy(
            src_ref=tx.at[slot, :, lanes],
            dst_ref=rx.at[mid, :, lanes],
            send_sem=tx_sem.at[mid, h],
            recv_sem=rx_sem.at[mid, h],
            device_id={"group": peer},
            device_id_type=MESH,
        )

    def slot_of(mid):
        chunk, kind = divmod(mid, 6)
        if chunk == 4:
            return 8 + kind
        return kind + (6 if chunk % 2 and kind < 2 else 0)

    def copies(mid):
        chunk, kind = divmod(mid, 6)
        return [copy_of(slot_of(mid), mid, kind, chunk // 4, h) for h in range(2)]

    pending = {}

    def send(mid, src, base, m):
        slot = slot_of(mid)
        if slot in pending:
            for c in copies(pending[slot]):
                c.wait_send()
        quantise(src, base, m, slot)
        for c in copies(mid):
            c.start()
        pending[slot] = mid

    def combine(acc, base, mids):
        for mid in mids:
            for c in copies(mid):
                c.wait_recv()
        scales = [
            jnp.exp2(rx[mid, HALF : HALF + 16, :].astype(jnp.int32).astype(F32)[:8]) * (1.0 / LEVELS)
            for mid in mids
        ]

        def tile(t, m):
            v = acc[at(base + t * 64, 64, 64), :].reshape(8, 8, ROWS)
            for mid, scale in zip(mids, scales):
                got = rx[mid, at(t * 64, 64, 64), :].astype(jnp.int32).astype(F32).reshape(8, 8, ROWS)
                v = v + got * scale[None]
            acc[at(base + t * 64, 64, 64), :] = v.reshape(64, ROWS)
            return jnp.maximum(m, jnp.max(jnp.abs(v), axis=0))

        return lax.fori_loop(0, HALF // 64, tile, jnp.zeros((8, ROWS), F32))

    def opposite_a(k):
        wait_step(k, 0)
        m = matmul(k, 0, A_TILES, tmp, 0)
        send(6 * k + OPP_A, tmp, 0, m)

    def opposite_b(k):
        m = matmul(k, 0, B_TILES, tmp, 0)
        send(6 * k + OPP_B, tmp, 0, m)

    def pure(k):
        wait_step(k, 1)
        wait_step(k, 2)
        m, _ = matmul_pair(k, B_TILES, tmp, 0, pdep, HALF)
        send(6 * k + PURE_B, tmp, 0, m)
        _, m = matmul_pair(k, A_TILES, pdep, 0, tmp, 0)
        send(6 * k + PURE_A, tmp, 0, m)

    def own(k):
        wait_step(k, 3)
        matmul(k, 3, A_TILES, pown, 0)
        matmul(k, 3, B_TILES, pown, HALF)

    def dependent(k):
        m = combine(pdep, 0, [6 * k + OPP_A])
        send(6 * k + DEP_A, pdep, 0, m)
        m = combine(pdep, HALF, [6 * k + OPP_B])
        send(6 * k + DEP_B, pdep, HALF, m)

    def complete(k):
        more_a = {0: [], 1: [24 + OPP_A], 2: [], 3: [24 + DEP_A, 24 + PURE_A]}[k]
        more_b = {0: [], 1: [], 2: [24 + OPP_B], 3: [24 + PURE_B, 24 + DEP_B]}[k]
        kind_a = {0: OPP_A, 1: DEP_A, 2: PURE_A}.get(k)
        kind_b = {0: OPP_B, 1: PURE_B, 2: DEP_B}.get(k)
        m = combine(pown, 0, [6 * k + DEP_A, 6 * k + PURE_A] + more_a)
        if k < 3:
            send(24 + kind_a, pown, 0, m)
        m = combine(pown, HALF, [6 * k + PURE_B, 6 * k + DEP_B] + more_b)
        if k < 3:
            send(24 + kind_b, pown, HALF, m)

    def post(src, dst, which, dy, dc, dx, dz):
        pltpu.make_async_remote_copy(
            src_ref=src,
            dst_ref=dst,
            send_sem=small_tx.at[which],
            recv_sem=small_rx.at[which],
            device_id={"replica": replica(dy, dc), "group": member(dx, dz)},
            device_id_type=MESH,
        ).start()

    def await_bytes(ref, sem):
        pltpu.make_async_copy(ref, ref, sem).wait()

    def all_reduce(src, core, total, chips, zs, xs_, result, first):
        length = src.shape[1]
        quarter = length // SIDE
        core_rows = at(rc * 32, 32, 32)
        my_rows = at(rc * 32 + ry * 8, 8, 8)

        def start():
            post(src.at[at((1 - rc) * 32, 32, 32), :], core, first, 0, 1, 0, 0)

        def along_y():
            await_bytes(core, small_rx.at[first])
            total[...] = src[core_rows, :] + core[...]
            for d in range(1, SIDE):
                post(total.at[at((ry + d) % SIDE * 8, 8, 8), :], chips.at[d - 1], first + 1, d, 0, 0, 0)

        def along_z():
            await_bytes(chips.at[pl.ds(0, 3)], small_rx.at[first + 1])
            chips[3] = (total[at(ry * 8, 8, 8), :] + chips[0]) + (chips[1] + chips[2])
            for d in range(SIDE):
                lanes = at((gz + d) % SIDE * quarter, quarter, 128)
                post(chips.at[3, :, lanes], zs.at[d], first + 2, 1, 0, 0, d)

        def along_x():
            await_bytes(zs.at[pl.ds(0, 4)], small_rx.at[first + 2])
            zs[4] = (zs[0] + zs[1]) + (zs[2] + zs[3])
            for d in range(1, SIDE):
                post(zs.at[4], xs_.at[gx], first + 3, 0, 0, d, 0)
            xs_[gx] = zs[4]

        def back_z():
            await_bytes(xs_.at[pl.ds(0, 3)], small_rx.at[first + 3])
            xs_[4] = (xs_[0] + xs_[1]) + (xs_[2] + xs_[3])
            rows = at(rc * 32 + (ry + SIDE - 1) % SIDE * 8, 8, 8)
            for d in range(SIDE):
                post(
                    xs_.at[4], result.at[rows, at(gz * quarter, quarter, 128)], first + 4, SIDE - 1, 0, 0, d
                )

        def back_y():
            await_bytes(result.at[pl.ds(0, 8), :], small_rx.at[first + 4])
            for d in range(1, SIDE):
                post(result.at[my_rows, :], result.at[my_rows, :], first + 5, d, 0, 0, 0)

        def back_core():
            await_bytes(result.at[pl.ds(0, 24), :], small_rx.at[first + 5])
            post(result.at[core_rows, :], result.at[core_rows, :], first + 6, 0, 1, 0, 0)

        def done():
            await_bytes(result.at[pl.ds(0, 32), :], small_rx.at[first + 6])

        def sent():
            await_bytes(result.at[pl.ds(0, 32), :], small_tx.at[first])
            await_bytes(result.at[pl.ds(0, 24), :], small_tx.at[first + 1])
            await_bytes(result.at[pl.ds(0, 8), :], small_tx.at[first + 2])
            await_bytes(xs_.at[pl.ds(0, 3)], small_tx.at[first + 3])
            await_bytes(result.at[pl.ds(0, 8), :], small_tx.at[first + 4])
            await_bytes(result.at[pl.ds(0, 24), :], small_tx.at[first + 5])
            await_bytes(result.at[pl.ds(0, 32), :], small_tx.at[first + 6])

        return start, along_y, along_z, along_x, back_z, back_y, back_core, done, sent

    def lanes_of(k, j):
        df, ds = ORDER[j], ORDER[k]
        return at(ROWS * member(df, ds), 128, 128), at(ROWS * member(ds, df) + 128, 128, 128)

    def make_factors():
        seed = seed_ref[0]
        for t in range(9):
            layer = t // 7
            q = factor_t(seed, 256 * (t - 7 * layer), 256, layer)
            q3[:, 256 * t : 256 * t + 256] = split3(q)

    def project():
        w_l = split3(fold3(dot_nn(q3[:, :FF], ut[:FF, :])))
        w_r = split3(fold3(dot_nn(q3[:, FF:], ut[FF:, :])))
        for k in range(SIDE):
            p_l = fold3(dot_nn(w_l, xs[k])) * (1.0 / 128)
            p_r = fold3(dot_nn(w_r, gs[k])) * (1.0 / 128)
            for j in range(SIDE):
                for part, lanes in enumerate(lanes_of(k, j)):
                    here = slice(256 * j + 128 * part, 256 * j + 128 * part + 128)
                    pt[:RANK, lanes] = p_l[:, here]
                    pt[RANK:, lanes] = p_r[:, here]

        mine = at(ROWS * group, ROWS, 128)
        for rows, columns in ((slice(0, RANK), slice(0, FF)), (slice(RANK, 64), slice(FF, W))):
            hi, low = split2(fb[:, columns])
            term = fold3(dot_nt(q3[:, columns], hi)) + fold3(dot_nt(q3[:, columns], low))
            pt[rows, mine] += term * (1.0 / 8)

    def back_project():
        y_l = jnp.zeros((96, TOK), F32)
        y_r = jnp.zeros((96, TOK), F32)
        for k in range(SIDE):
            parts = []
            for j in range(SIDE):
                for lanes in lanes_of(k, j):
                    parts.append(pall[:, lanes])
            p = jnp.concatenate(parts, axis=1)
            y_l = y_l + dot_nt(split3(p[:RANK]), xs[k])
            y_r = y_r + dot_nt(split3(p[RANK:]), gs[k])
        y_l = split3(fold3(y_l) * (1.0 / 128))
        y_r = split3(fold3(y_r) * (1.0 / 128))
        p = pall[:, at(ROWS * group, ROWS, 128)] * (1.0 / 8)
        p_l, p_r = split3(p[:RANK]), split3(p[RANK:])

        def piece(y, p3, columns):
            hi, low = split2(fb[:, columns])
            return fold3(dot_nt(y, ut[columns, :])) + (fold3(dot_nn(p3, hi)) + fold3(dot_nn(p3, low)))

        bt[:RANK, :HALF] = piece(y_l, p_l, slice(0, HALF))
        bt[RANK:, 0:640] = piece(y_l, p_l, slice(HALF, FF))
        bt[RANK:, 640:HALF] = piece(y_r, p_r, slice(FF, W))
        bt[:, HALF:] = jnp.zeros((64, BLEN - HALF), F32)

    def factors():
        gram_l = dot_nt_full(pall[:RANK, :], pall[:RANK, :])
        gram_r = dot_nt_full(pall[RANK:, :], pall[RANK:, :])
        return inverse_factor((gram_l, gram_r))

    def quad(v, last):
        hi, low = split2(v)
        return jnp.concatenate([hi, hi, low, low] if last else [hi, low, hi, low], axis=0)

    def bases(t_l, t_r, lanes):
        return jnp.concatenate(
            [
                quad(apply_factor(t_l, pall[:RANK, lanes]), True),
                quad(apply_factor(t_r, pall[RANK:, lanes]), True),
            ],
            axis=0,
        )

    def decompress(t_l, t_r):
        mine = bases(t_l, t_r, at(ROWS * group, ROWS, 128)).T
        pieces = (
            (t_l, slice(0, RANK), 0, HALF, 0),
            (t_l, slice(RANK, 64), 0, 640, HALF),
            (t_r, slice(RANK, 64), 640, HALF, HALF),
        )
        for t, rows, lo, hi, base in pieces:
            b4 = quad(apply_factor(t, ball[rows, lo:hi]), False)
            none = jnp.zeros_like(b4)
            left = base + lo < FF
            both = jnp.concatenate([b4, none] if left else [none, b4], axis=0)
            fb[:, base + lo : base + hi] -= dot_nn(mine, both)
            bk4[base + lo : base + hi, :] = both.T
        width = W // REP
        chosen = bk4[at(rep * width, width, 16), :]
        for t in range(4):
            lanes = slice(1024 * t, 1024 * t + 1024)
            uout[:, lanes] = dot_nn(chosen, bases(t_l, t_r, lanes)).astype(BF16)
        pltpu.make_async_copy(uout, upd_hbm, out_sem.at[0]).start()

    p_steps = all_reduce(pt, pc, ps, py, pz, px, pall, 0)
    b_steps = all_reduce(bt, bc, bs, by, bz, bx, ball, 7)

    load_a.wait()
    transpose_u(0, (384, 384, 384))
    load_b.start()
    load_c.start()
    pl.semaphore_wait(barrier, 15)
    opposite_a(0)
    load_b.wait()
    load_c.wait()
    transpose_u(HALF, (256, 384, 256, 256))
    opposite_b(0)
    pure(0)
    make_factors()
    for k in range(SIDE):
        for j in range(SIDE):
            wait_step(k, j)
    pltpu.make_async_copy(fb_hbm, fb, load_fb).wait()
    project()
    p_steps[0]()
    own(0)
    p_steps[1]()
    opposite_a(1)
    opposite_b(1)
    dependent(0)
    pure(1)
    p_steps[2]()
    dependent(1)
    p_steps[3]()
    complete(0)
    opposite_a(2)
    opposite_b(2)
    own(1)
    p_steps[4]()
    pure(2)
    p_steps[5]()
    dependent(2)
    p_steps[6]()
    complete(1)
    p_steps[7]()
    back_project()
    b_steps[0]()
    own(2)
    b_steps[1]()
    opposite_a(3)
    opposite_b(3)
    b_steps[2]()
    pure(3)
    b_steps[3]()
    dependent(3)
    t_l, t_r = factors()
    complete(2)
    b_steps[4]()
    own(3)
    b_steps[5]()
    b_steps[6]()
    b_steps[7]()
    decompress(t_l, t_r)
    complete(3)

    for t in range(9):
        columns = slice(256 * t, 256 * t + 256)
        fb[:, columns] += pown[columns, :].T * (1.0 / GROUP)
    pltpu.make_async_copy(fb, new_hbm, out_sem.at[1]).start()

    for slot in pending:
        for c in copies(pending[slot]):
            c.wait_send()
    p_steps[8]()
    b_steps[8]()
    pltpu.make_async_copy(uout, upd_hbm, out_sem.at[0]).wait()
    pltpu.make_async_copy(fb, new_hbm, out_sem.at[1]).wait()


def small_buffers(length):
    quarter = length // SIDE
    shapes = (
        (64, length), (32, length), (32, length), (4, 8, length), (5, 8, quarter), (5, 8, quarter), (64, length)
    )
    return [pltpu.VMEM(shape, F32) for shape in shapes]


def on_device(layer_input, up_cotangent, attn_values, resid_cotangent, feedback, start_seed):
    hbm = pl.BlockSpec(memory_space=pl.ANY)
    dma = pltpu.SemaphoreType.DMA
    new_feedback, update = pl.pallas_call(
        kernel,
        out_shape=(
            jax.ShapeDtypeStruct((ROWS, W), F32),
            jax.ShapeDtypeStruct((W // REP, D), BF16),
        ),
        in_specs=[hbm] * 5 + [pl.BlockSpec(memory_space=pltpu.SMEM)],
        out_specs=(hbm, hbm),
        scratch_shapes=[
            pltpu.VMEM((SIDE, TOK, SIDE * ROWS), BF16),
            pltpu.VMEM((SIDE, TOK, SIDE * ROWS), BF16),
            pltpu.VMEM((W, TOK), BF16),
            pltpu.VMEM((TOK, HALF), BF16),
            pltpu.VMEM((HALF, ROWS), F32),
            pltpu.VMEM((W, ROWS), F32),
            pltpu.VMEM((W, ROWS), F32),
            pltpu.VMEM((14, HALF + 16, ROWS), jnp.int16),
            pltpu.VMEM((30, HALF + 16, ROWS), jnp.int16),
            pltpu.VMEM((ROWS, W), F32),
            pltpu.VMEM((96, W), BF16),
            *small_buffers(D),
            *small_buffers(BLEN),
            pltpu.VMEM((W, 256), BF16),
            pltpu.VMEM((W // REP, D), BF16),
            dma((GROUP,)),
            dma((GROUP,)),
            dma((3,)),
            dma,
            dma((2,)),
            dma((30, 2)),
            dma((30, 2)),
            dma((14,)),
            dma((14,)),
        ],
        compiler_params=pltpu.CompilerParams(
            collective_id=0, has_side_effects=True, vmem_limit_bytes=64 * 1024 * 1024 - 256 * 1024
        ),
        cost_estimate=pl.CostEstimate(flops=2 * TOK * D * W, bytes_accessed=21_000_000, transcendentals=0),
    )(layer_input, up_cotangent, attn_values, resid_cotangent, feedback[0], start_seed)
    return (update.T, new_feedback[None])


def solution(mesh):
    in_specs = (
        P(("replica", "group"), None),
        P(("replica", "group"), None),
        P(("replica", "group"), None),
        P(("replica", "group"), None),
        P("replica", "group", None),
        P(),
    )
    out_specs = (P(None, "replica"), P("replica", "group", None))
    return jax.shard_map(
        on_device, mesh=mesh, in_specs=in_specs, out_specs=out_specs, check_vma=False
    )
```

```python
import jax
import jax.numpy as jnp
from jax import lax
from jax.experimental import pallas as pl
from jax.experimental.pallas import tpu as pltpu
from jax.sharding import PartitionSpec as P

RANK = 32
TOK = 768
D = 4096
FF = 1792
HD = 512
W = FF + HD
HALF = W // 2
ROWS = 256
SIDE = 4
GROUP = 16
REP = 8
BLEN = 1536
LEVELS = 32700.0
ORDER = (2, 1, 3, 0)
MESH = pl.DeviceIdType.MESH
F32 = jnp.float32
BF16 = jnp.bfloat16
OPP_A, OPP_B, PURE_B, PURE_A, DEP_A, DEP_B = range(6)
RIGHTWARD = (True, False, True, False, True, False)


def modulo(v):
    r = v - jnp.floor(v * (1.0 / 65521.0)) * 65521.0
    r = jnp.where(r < 0.0, r + 65521.0, r)
    return jnp.where(r >= 65521.0, r - 65521.0, r)


def factor_t(seed, first, count, layer):
    positions = lax.broadcasted_iota(jnp.int32, (RANK, count), 1) + first
    columns = lax.broadcasted_iota(jnp.int32, (RANK, count), 0)
    base = (seed % 65521) * 31 + layer * 4099 + 12345
    mixed = modulo((base + positions * 977 + columns * 7919).astype(F32)).astype(jnp.int32)
    folded = (mixed & 255) * (mixed >> 8)
    final = modulo((folded * 181 + mixed).astype(F32))
    return (final / 65521.0 - 0.5) * 3.4


def split3(v):
    hi = v.astype(BF16)
    rest = v - hi.astype(F32)
    mid = rest.astype(BF16)
    low = (rest - mid.astype(F32)).astype(BF16)
    return jnp.concatenate([hi, mid, low], axis=0)


def split2(v):
    hi = v.astype(BF16)
    return hi, (v - hi.astype(F32)).astype(BF16)


def fold3(v):
    return (v[64:96] + v[32:64]) + v[0:32]


def dot_nn(a, b):
    return lax.dot_general(a, b, (((1,), (0,)), ((), ())), preferred_element_type=F32)


def dot_nt(a, b):
    return lax.dot_general(a, b, (((1,), (1,)), ((), ())), preferred_element_type=F32)


def dot_tn(a, b):
    return lax.dot_general(a, b, (((0,), (0,)), ((), ())), preferred_element_type=F32)


def dot_nt_full(a, b):
    return lax.dot_general(
        a, b, (((1,), (1,)), ((), ())), precision=lax.Precision.HIGHEST, preferred_element_type=F32
    )


def peak8(v):
    return jnp.max(jnp.abs(v).reshape(v.shape[0] // 8, 8, v.shape[1]), axis=0)


def at(start, size, step):
    return pl.ds(pl.multiple_of(start, step), size)


def pieces3(v):
    hi = v.astype(BF16)
    rest = v - hi.astype(F32)
    mid = rest.astype(BF16)
    return hi, mid, (rest - mid.astype(F32)).astype(BF16)


def apply_factor(t_t, v):
    hi, mid, low = pieces3(t_t)
    left = jnp.concatenate([hi, hi, hi, mid, mid, low], axis=0)
    hi, mid, low = pieces3(v)
    return dot_tn(left, jnp.concatenate([hi, mid, low, hi, mid, hi], axis=0))


def eliminate(state, first, last):
    row = lax.broadcasted_iota(jnp.int32, (RANK, RANK), 0)
    lane = lax.broadcasted_iota(jnp.int32, (RANK, RANK), 1)

    def step(j, state):
        out = []
        for a, b in state:
            a_row = jnp.sum(jnp.where(row == j, a, 0.0), axis=0, keepdims=True)
            pivot = jnp.sum(jnp.where(lane[:1] == j, a_row, 0.0), axis=1, keepdims=True)
            a_col = jnp.sum(jnp.where(lane == j, a, 0.0), axis=1, keepdims=True)
            b_col = jnp.sum(jnp.where(lane == j, b, 0.0), axis=1, keepdims=True)
            factor = jnp.where(lane[:1] > j, a_row / pivot, 0.0)
            out.append((a - a_col * factor, b - b_col * factor))
        return tuple(out)

    return lax.fori_loop(first, last, step, state)


def identity():
    row = lax.broadcasted_iota(jnp.int32, (RANK, RANK), 0)
    lane = lax.broadcasted_iota(jnp.int32, (RANK, RANK), 1)
    return jnp.where(row == lane, 1.0, 0.0).astype(F32)


def scaled(state):
    eye = identity()
    return [b * (1.0 / jnp.sqrt(jnp.sum(a * eye, axis=0, keepdims=True))) for a, b in state]


def kernel(
    x_hbm, u_hbm, a_hbm, g_hbm, fb_hbm, seed_ref,
    new_hbm, upd_hbm,
    xs, gs, ut, ustg, tmp, pdep, pown, tx, rx, fb, q3,
    pt, pc, ps, py, pz, px, pall,
    bt, bc, bs, by, bz, bx, ball, bk4, uout,
    load_x, load_g, load_u, load_fb, out_sem,
    tx_sem, rx_sem, small_tx, small_rx,
):
    group = lax.axis_index("group")
    rep = lax.axis_index("replica")
    gx = group // SIDE
    gz = group % SIDE
    ry = rep // 2
    rc = rep % 2

    def member(dx, dz):
        return (gx + dx) % SIDE * SIDE + (gz + dz) % SIDE

    def replica(dy, dc):
        return (ry + dy) % SIDE * 2 + (rc + dc) % 2

    def load_step(k, j):
        df, ds = ORDER[j], ORDER[k]
        low = at(ROWS * member(df, ds), 128, 128)
        high = at(ROWS * member(ds, df) + 128, 128, 128)
        for src, dst, sem in ((x_hbm, xs, load_x), (g_hbm, gs, load_g)):
            for part, lanes in enumerate((low, high)):
                pltpu.make_async_copy(
                    src.at[:, lanes], dst.at[k, :, pl.ds(256 * j + 128 * part, 128)], sem.at[4 * k + j]
                ).start()

    load_a = pltpu.make_async_copy(u_hbm.at[:, pl.ds(0, HALF)], ustg, load_u.at[0])
    load_b = pltpu.make_async_copy(
        u_hbm.at[:, pl.ds(HALF, FF - HALF)], ustg.at[:, pl.ds(0, FF - HALF)], load_u.at[1]
    )
    load_c = pltpu.make_async_copy(a_hbm, ustg.at[:, pl.ds(FF - HALF, HD)], load_u.at[2])
    load_a.start()
    for k in range(SIDE):
        for j in range(SIDE):
            load_step(k, j)
    pltpu.make_async_copy(fb_hbm, fb, load_fb).start()
    loaded = set()

    def wait_step(k, j):
        if (k, j) in loaded:
            return
        loaded.add((k, j))
        for ref, sem in ((xs, load_x), (gs, load_g)):
            part = ref.at[k, :, pl.ds(256 * j, 256)]
            pltpu.make_async_copy(part, part, sem.at[4 * k + j]).wait()

    barrier = pltpu.get_barrier_semaphore()

    def greet(dy, dc, dx, dz):
        pl.semaphore_signal(
            barrier,
            inc=1,
            device_id={"replica": replica(dy, dc), "group": member(dx, dz)},
            device_id_type=MESH,
        )

    greet(0, 1, 0, 0)
    for d in range(1, SIDE):
        greet(d, 0, 0, 0)
        greet(1, 0, 0, d)
        greet(SIDE - 1, 0, 0, d)
        greet(0, 0, d, 0)
    greet(0, 0, 0, 1)
    greet(0, 0, 0, SIDE - 1)

    def transpose_u(base, sizes):
        start = 0
        for size in sizes:
            ut[base + start : base + start + size, :] = ustg[:, start : start + size].T
            start += size

    A_TILES = ((0, HALF, xs),)
    B_TILES = ((HALF, FF - HALF, xs), (FF, HD, gs))

    def products(k, lanes, tiles):
        row = 0
        for start, size, source in tiles:
            yield row, size, dot_nn(ut[start : start + size, :], source[k, :, lanes])
            row += size

    def matmul(k, j, tiles, dst, base):
        peak = jnp.zeros((8, ROWS), F32)
        for row, size, value in products(k, slice(256 * j, 256 * j + 256), tiles):
            dst[base + row : base + row + size, :] = value
            peak = jnp.maximum(peak, peak8(value))
        return peak

    def matmul_pair(k, tiles, dst_1, base_1, dst_2, base_2):
        peak = jnp.zeros((8, 2 * ROWS), F32)
        for row, size, value in products(k, slice(256, 768), tiles):
            dst_1[base_1 + row : base_1 + row + size, :] = value[:, :ROWS]
            dst_2[base_2 + row : base_2 + row + size, :] = value[:, ROWS:]
            peak = jnp.maximum(peak, peak8(value))
        return peak[:, :ROWS], peak[:, ROWS:]

    def quantise(src, base, m, slot):
        peak = jnp.maximum(jnp.max(m, axis=0, keepdims=True), 1e-30)
        power = jnp.ceil(jnp.log2(peak))
        scale = jnp.exp2(-power) * LEVELS

        @pl.loop(0, HALF // 64)
        def _(t):
            v = src[at(base + t * 64, 64, 64), :] * scale
            tx[slot, at(t * 64, 64, 64), :] = jnp.round(v).astype(jnp.int32).astype(jnp.int16)

        tx[slot, HALF : HALF + 16, :] = jnp.broadcast_to(power, (16, ROWS)).astype(jnp.int32).astype(jnp.int16)

    def copy_of(slot, mid, kind, stage, h):
        lanes = pl.ds(128 * h, 128)
        along_x = (h == 0) == (stage == 0)
        step = 1 if RIGHTWARD[kind] else SIDE - 1
        peer = member(step, 0) if along_x else member(0, step)
        return pltpu.make_async_remote_copy(
            src_ref=tx.at[slot, :, lanes],
            dst_ref=rx.at[mid, :, lanes],
            send_sem=tx_sem.at[mid, h],
            recv_sem=rx_sem.at[mid, h],
            device_id={"group": peer},
            device_id_type=MESH,
        )

    def slot_of(mid):
        chunk, kind = divmod(mid, 6)
        if chunk == 4:
            return 8 + kind
        return kind + (6 if chunk % 2 and kind < 2 else 0)

    def copies(mid):
        chunk, kind = divmod(mid, 6)
        return [copy_of(slot_of(mid), mid, kind, chunk // 4, h) for h in range(2)]

    pending = {}

    def send(mid, src, base, m, held=()):
        slot = slot_of(mid)
        if slot in pending:
            for c in copies(pending[slot]):
                c.wait_send()
        quantise(src, base, m, slot)
        for h, c in enumerate(copies(mid)):
            if h not in held:
                c.start()
        pending[slot] = mid

    def release(mid, h):
        copies(mid)[h].start()

    def combine(acc, base, mids):
        for mid in mids:
            for c in copies(mid):
                c.wait_recv()
        scales = [
            jnp.exp2(rx[mid, HALF : HALF + 16, :].astype(jnp.int32).astype(F32)[:8]) * (1.0 / LEVELS)
            for mid in mids
        ]

        def tile(t, m):
            v = acc[at(base + t * 64, 64, 64), :].reshape(8, 8, ROWS)
            for mid, scale in zip(mids, scales):
                got = rx[mid, at(t * 64, 64, 64), :].astype(jnp.int32).astype(F32).reshape(8, 8, ROWS)
                v = v + got * scale[None]
            acc[at(base + t * 64, 64, 64), :] = v.reshape(64, ROWS)
            return jnp.maximum(m, jnp.max(jnp.abs(v), axis=0))

        return lax.fori_loop(0, HALF // 64, tile, jnp.zeros((8, ROWS), F32))

    def opposite_a(k, held=()):
        wait_step(k, 0)
        m = matmul(k, 0, A_TILES, tmp, 0)
        send(6 * k + OPP_A, tmp, 0, m, held)

    def opposite_b(k):
        wait_step(k, 0)
        m = matmul(k, 0, B_TILES, tmp, 0)
        send(6 * k + OPP_B, tmp, 0, m)

    def pure_b(k, held=()):
        wait_step(k, 1)
        wait_step(k, 2)
        m, _ = matmul_pair(k, B_TILES, tmp, 0, pdep, HALF)
        send(6 * k + PURE_B, tmp, 0, m, held)

    def pure_a(k):
        wait_step(k, 1)
        wait_step(k, 2)
        _, m = matmul_pair(k, A_TILES, pdep, 0, tmp, 0)
        send(6 * k + PURE_A, tmp, 0, m)

    def own(k):
        wait_step(k, 3)
        matmul(k, 3, A_TILES, pown, 0)
        matmul(k, 3, B_TILES, pown, HALF)

    def dependent_a(k):
        m = combine(pdep, 0, [6 * k + OPP_A])
        send(6 * k + DEP_A, pdep, 0, m)

    def dependent_b(k):
        m = combine(pdep, HALF, [6 * k + OPP_B])
        send(6 * k + DEP_B, pdep, HALF, m)

    def complete_a(k):
        more = {0: [], 1: [24 + OPP_A], 2: [], 3: [24 + DEP_A, 24 + PURE_A]}[k]
        m = combine(pown, 0, [6 * k + DEP_A, 6 * k + PURE_A] + more)
        if k < 3:
            send(24 + (OPP_A, DEP_A, PURE_A)[k], pown, 0, m)

    def complete_b(k):
        more = {0: [], 1: [], 2: [24 + OPP_B], 3: [24 + PURE_B, 24 + DEP_B]}[k]
        m = combine(pown, HALF, [6 * k + PURE_B, 6 * k + DEP_B] + more)
        if k < 3:
            send(24 + (OPP_B, PURE_B, DEP_B)[k], pown, HALF, m)

    def post(src, dst, which, dy, dc, dx, dz):
        pltpu.make_async_remote_copy(
            src_ref=src,
            dst_ref=dst,
            send_sem=small_tx.at[which],
            recv_sem=small_rx.at[which],
            device_id={"replica": replica(dy, dc), "group": member(dx, dz)},
            device_id_type=MESH,
        ).start()

    def await_bytes(ref, sem):
        pltpu.make_async_copy(ref, ref, sem).wait()

    def all_reduce(src, core, total, chips, zs, xs_, result, first):
        length = src.shape[1]
        quarter = length // SIDE
        core_rows = at(rc * 32, 32, 32)
        my_rows = at(rc * 32 + ry * 8, 8, 8)

        def start():
            post(src.at[at((1 - rc) * 32, 32, 32), :], core, first, 0, 1, 0, 0)

        def along_y():
            await_bytes(core, small_rx.at[first])
            total[...] = src[core_rows, :] + core[...]
            for d in range(1, SIDE):
                post(total.at[at((ry + d) % SIDE * 8, 8, 8), :], chips.at[d - 1], first + 1, d, 0, 0, 0)

        def along_z():
            await_bytes(chips.at[pl.ds(0, 3)], small_rx.at[first + 1])
            chips[3] = (total[at(ry * 8, 8, 8), :] + chips[0]) + (chips[1] + chips[2])
            for d in range(SIDE):
                lanes = at((gz + d) % SIDE * quarter, quarter, 128)
                post(chips.at[3, :, lanes], zs.at[d], first + 2, 1, 0, 0, d)

        def along_x():
            await_bytes(zs.at[pl.ds(0, 4)], small_rx.at[first + 2])
            zs[4] = (zs[0] + zs[1]) + (zs[2] + zs[3])
            for d in range(1, SIDE):
                post(zs.at[4], xs_.at[gx], first + 3, 0, 0, d, 0)
            xs_[gx] = zs[4]

        def back_z():
            await_bytes(xs_.at[pl.ds(0, 3)], small_rx.at[first + 3])
            xs_[4] = (xs_[0] + xs_[1]) + (xs_[2] + xs_[3])
            rows = at(rc * 32 + (ry + SIDE - 1) % SIDE * 8, 8, 8)
            for d in range(SIDE):
                post(
                    xs_.at[4], result.at[rows, at(gz * quarter, quarter, 128)], first + 4, SIDE - 1, 0, 0, d
                )

        def back_y():
            await_bytes(result.at[pl.ds(0, 8), :], small_rx.at[first + 4])
            for d in range(1, SIDE):
                post(result.at[my_rows, :], result.at[my_rows, :], first + 5, d, 0, 0, 0)

        def back_core():
            await_bytes(result.at[pl.ds(0, 24), :], small_rx.at[first + 5])
            post(result.at[core_rows, :], result.at[core_rows, :], first + 6, 0, 1, 0, 0)

        def done():
            await_bytes(result.at[pl.ds(0, 32), :], small_rx.at[first + 6])

        def sent():
            await_bytes(result.at[pl.ds(0, 32), :], small_tx.at[first])
            await_bytes(result.at[pl.ds(0, 24), :], small_tx.at[first + 1])
            await_bytes(result.at[pl.ds(0, 8), :], small_tx.at[first + 2])
            await_bytes(xs_.at[pl.ds(0, 3)], small_tx.at[first + 3])
            await_bytes(result.at[pl.ds(0, 8), :], small_tx.at[first + 4])
            await_bytes(result.at[pl.ds(0, 24), :], small_tx.at[first + 5])
            await_bytes(result.at[pl.ds(0, 32), :], small_tx.at[first + 6])

        return start, along_y, along_z, along_x, back_z, back_y, back_core, done, sent

    def lanes_of(k, j):
        df, ds = ORDER[j], ORDER[k]
        return at(ROWS * member(df, ds), 128, 128), at(ROWS * member(ds, df) + 128, 128, 128)

    def make_factors():
        seed = seed_ref[0]
        for t in range(9):
            layer = t // 7
            q = factor_t(seed, 256 * (t - 7 * layer), 256, layer)
            q3[:, 256 * t : 256 * t + 256] = split3(q)

    def project():
        w_l = split3(fold3(dot_nn(q3[:, :FF], ut[:FF, :])))
        w_r = split3(fold3(dot_nn(q3[:, FF:], ut[FF:, :])))
        for k in range(SIDE):
            p_l = fold3(dot_nn(w_l, xs[k])) * (1.0 / 128)
            p_r = fold3(dot_nn(w_r, gs[k])) * (1.0 / 128)
            for j in range(SIDE):
                for part, lanes in enumerate(lanes_of(k, j)):
                    here = slice(256 * j + 128 * part, 256 * j + 128 * part + 128)
                    pt[:RANK, lanes] = p_l[:, here]
                    pt[RANK:, lanes] = p_r[:, here]

        mine = at(ROWS * group, ROWS, 128)
        for rows, columns in ((slice(0, RANK), slice(0, FF)), (slice(RANK, 64), slice(FF, W))):
            hi, low = split2(fb[:, columns])
            term = fold3(dot_nt(q3[:, columns], hi)) + fold3(dot_nt(q3[:, columns], low))
            pt[rows, mine] += term * (1.0 / 8)

    def back_project():
        y_l = jnp.zeros((96, TOK), F32)
        y_r = jnp.zeros((96, TOK), F32)
        for k in range(SIDE):
            parts = []
            for j in range(SIDE):
                for lanes in lanes_of(k, j):
                    parts.append(pall[:, lanes])
            p = jnp.concatenate(parts, axis=1)
            y_l = y_l + dot_nt(split3(p[:RANK]), xs[k])
            y_r = y_r + dot_nt(split3(p[RANK:]), gs[k])
        y_l = split3(fold3(y_l) * (1.0 / 128))
        y_r = split3(fold3(y_r) * (1.0 / 128))
        p = pall[:, at(ROWS * group, ROWS, 128)] * (1.0 / 8)
        p_l, p_r = split3(p[:RANK]), split3(p[RANK:])

        def piece(y, p3, columns):
            hi, low = split2(fb[:, columns])
            return fold3(dot_nt(y, ut[columns, :])) + (fold3(dot_nn(p3, hi)) + fold3(dot_nn(p3, low)))

        bt[:RANK, :HALF] = piece(y_l, p_l, slice(0, HALF))
        bt[RANK:, 0:640] = piece(y_l, p_l, slice(HALF, FF))
        bt[RANK:, 640:HALF] = piece(y_r, p_r, slice(FF, W))
        bt[:, HALF:] = jnp.zeros((64, BLEN - HALF), F32)

    def grams():
        eye = identity()
        return tuple(
            (dot_nt_full(pall[rows, :], pall[rows, :]), eye) for rows in (slice(0, RANK), slice(RANK, 64))
        )

    def quad(v, last):
        hi, low = split2(v)
        return jnp.concatenate([hi, hi, low, low] if last else [hi, low, hi, low], axis=0)

    def bases(t_l, t_r, lanes):
        return jnp.concatenate(
            [
                quad(apply_factor(t_l, pall[:RANK, lanes]), True),
                quad(apply_factor(t_r, pall[RANK:, lanes]), True),
            ],
            axis=0,
        )

    def decompress(t_l, t_r):
        mine = bases(t_l, t_r, at(ROWS * group, ROWS, 128)).T
        pieces = (
            (t_l, slice(0, RANK), 0, HALF, 0),
            (t_l, slice(RANK, 64), 0, 640, HALF),
            (t_r, slice(RANK, 64), 640, HALF, HALF),
        )
        for t, rows, lo, hi, base in pieces:
            b4 = quad(apply_factor(t, ball[rows, lo:hi]), False)
            none = jnp.zeros_like(b4)
            left = base + lo < FF
            both = jnp.concatenate([b4, none] if left else [none, b4], axis=0)
            fb[:, base + lo : base + hi] -= dot_nn(mine, both)
            bk4[base + lo : base + hi, :] = both.T
        width = W // REP
        chosen = bk4[at(rep * width, width, 16), :]
        for t in range(4):
            lanes = slice(1024 * t, 1024 * t + 1024)
            uout[:, lanes] = dot_nn(chosen, bases(t_l, t_r, lanes)).astype(BF16)
        pltpu.make_async_copy(uout, upd_hbm, out_sem.at[0]).start()

    p_steps = all_reduce(pt, pc, ps, py, pz, px, pall, 0)
    b_steps = all_reduce(bt, bc, bs, by, bz, bx, ball, 7)

    load_a.wait()
    transpose_u(0, (384, 384, 384))
    load_b.start()
    load_c.start()
    pl.semaphore_wait(barrier, 15)
    opposite_a(0)
    load_b.wait()
    load_c.wait()
    transpose_u(HALF, (256, 384, 256, 256))
    opposite_b(0)
    pure_b(0)
    pure_a(0)
    make_factors()
    for k in range(SIDE):
        for j in range(SIDE):
            wait_step(k, j)
    pltpu.make_async_copy(fb_hbm, fb, load_fb).wait()
    project()
    p_steps[0]()
    own(0)
    p_steps[1]()
    opposite_a(1)
    opposite_b(1)
    dependent_a(0)
    dependent_b(0)
    pure_b(1)
    pure_a(1)
    p_steps[2]()
    p_steps[3]()
    dependent_a(1)
    dependent_b(1)
    complete_a(0)
    complete_b(0)
    opposite_a(2)
    opposite_b(2)
    own(1)
    p_steps[4]()
    pure_b(2)
    pure_a(2)
    p_steps[5]()
    dependent_a(2)
    dependent_b(2)
    p_steps[6]()
    complete_a(1)
    complete_b(1)
    p_steps[7]()
    back_project()
    b_steps[0]()
    opposite_b(3)
    opposite_a(3, held=(0,))
    b_steps[1]()
    own(2)
    pure_a(3)
    pure_b(3, held=(0,))
    state = eliminate(grams(), 0, 8)
    b_steps[2]()
    state = eliminate(state, 8, 20)
    b_steps[3]()
    release(18 + OPP_A, 0)
    release(18 + PURE_B, 0)
    complete_b(2)
    complete_a(2)
    state = eliminate(state, 20, RANK)
    t_l, t_r = scaled(state)
    b_steps[4]()
    own(3)
    dependent_b(3)
    b_steps[5]()
    b_steps[6]()
    dependent_a(3)
    b_steps[7]()
    decompress(t_l, t_r)
    complete_b(3)
    complete_a(3)

    for t in range(9):
        columns = slice(256 * t, 256 * t + 256)
        fb[:, columns] += pown[columns, :].T * (1.0 / GROUP)
    pltpu.make_async_copy(fb, new_hbm, out_sem.at[1]).start()

    for slot in pending:
        for c in copies(pending[slot]):
            c.wait_send()
    p_steps[8]()
    b_steps[8]()
    pltpu.make_async_copy(uout, upd_hbm, out_sem.at[0]).wait()
    pltpu.make_async_copy(fb, new_hbm, out_sem.at[1]).wait()


def small_buffers(length):
    quarter = length // SIDE
    shapes = (
        (64, length), (32, length), (32, length), (4, 8, length), (5, 8, quarter), (5, 8, quarter), (64, length)
    )
    return [pltpu.VMEM(shape, F32) for shape in shapes]


def on_device(layer_input, up_cotangent, attn_values, resid_cotangent, feedback, start_seed):
    hbm = pl.BlockSpec(memory_space=pl.ANY)
    dma = pltpu.SemaphoreType.DMA
    new_feedback, update = pl.pallas_call(
        kernel,
        out_shape=(
            jax.ShapeDtypeStruct((ROWS, W), F32),
            jax.ShapeDtypeStruct((W // REP, D), BF16),
        ),
        in_specs=[hbm] * 5 + [pl.BlockSpec(memory_space=pltpu.SMEM)],
        out_specs=(hbm, hbm),
        scratch_shapes=[
            pltpu.VMEM((SIDE, TOK, SIDE * ROWS), BF16),
            pltpu.VMEM((SIDE, TOK, SIDE * ROWS), BF16),
            pltpu.VMEM((W, TOK), BF16),
            pltpu.VMEM((TOK, HALF), BF16),
            pltpu.VMEM((HALF, ROWS), F32),
            pltpu.VMEM((W, ROWS), F32),
            pltpu.VMEM((W, ROWS), F32),
            pltpu.VMEM((14, HALF + 16, ROWS), jnp.int16),
            pltpu.VMEM((30, HALF + 16, ROWS), jnp.int16),
            pltpu.VMEM((ROWS, W), F32),
            pltpu.VMEM((96, W), BF16),
            *small_buffers(D),
            *small_buffers(BLEN),
            pltpu.VMEM((W, 256), BF16),
            pltpu.VMEM((W // REP, D), BF16),
            dma((GROUP,)),
            dma((GROUP,)),
            dma((3,)),
            dma,
            dma((2,)),
            dma((30, 2)),
            dma((30, 2)),
            dma((14,)),
            dma((14,)),
        ],
        compiler_params=pltpu.CompilerParams(
            collective_id=0, has_side_effects=True, vmem_limit_bytes=64 * 1024 * 1024 - 256 * 1024
        ),
        cost_estimate=pl.CostEstimate(flops=2 * TOK * D * W, bytes_accessed=21_000_000, transcendentals=0),
    )(layer_input, up_cotangent, attn_values, resid_cotangent, feedback[0], start_seed)
    return (update.T, new_feedback[None])


def solution(mesh):
    in_specs = (
        P(("replica", "group"), None),
        P(("replica", "group"), None),
        P(("replica", "group"), None),
        P(("replica", "group"), None),
        P("replica", "group", None),
        P(),
    )
    out_specs = (P(None, "replica"), P("replica", "group", None))
    return jax.shard_map(
        on_device, mesh=mesh, in_specs=in_specs, out_specs=out_specs, check_vma=False
    )
```

```python
import jax
import jax.numpy as jnp
from jax import lax
from jax.experimental import pallas as pl
from jax.experimental.pallas import tpu as pltpu
from jax.sharding import PartitionSpec as P

RANK = 32
TOK = 768
D = 4096
FF = 1792
HD = 512
W = FF + HD
HALF = W // 2
ROWS = 256
SIDE = 4
GROUP = 16
REP = 8
BLEN = 1536
LEVELS = 32700.0
ORDER = (2, 1, 3, 0)
MESH = pl.DeviceIdType.MESH
F32 = jnp.float32
BF16 = jnp.bfloat16
OPP_A, OPP_B, PURE_B, PURE_A, DEP_A, DEP_B = range(6)
RIGHTWARD = (True, False, True, False, True, False)


def modulo(v):
    r = v - jnp.floor(v * (1.0 / 65521.0)) * 65521.0
    r = jnp.where(r < 0.0, r + 65521.0, r)
    return jnp.where(r >= 65521.0, r - 65521.0, r)


def factor_t(seed, first, count, layer):
    positions = lax.broadcasted_iota(jnp.int32, (RANK, count), 1) + first
    columns = lax.broadcasted_iota(jnp.int32, (RANK, count), 0)
    base = (seed % 65521) * 31 + layer * 4099 + 12345
    mixed = modulo((base + positions * 977 + columns * 7919).astype(F32)).astype(jnp.int32)
    folded = (mixed & 255) * (mixed >> 8)
    final = modulo((folded * 181 + mixed).astype(F32))
    return (final / 65521.0 - 0.5) * 3.4


def split3(v):
    hi = v.astype(BF16)
    rest = v - hi.astype(F32)
    mid = rest.astype(BF16)
    low = (rest - mid.astype(F32)).astype(BF16)
    return jnp.concatenate([hi, mid, low], axis=0)


def split2(v):
    hi = v.astype(BF16)
    return hi, (v - hi.astype(F32)).astype(BF16)


def fold3(v):
    return (v[64:96] + v[32:64]) + v[0:32]


def dot_nn(a, b):
    return lax.dot_general(a, b, (((1,), (0,)), ((), ())), preferred_element_type=F32)


def dot_nt(a, b):
    return lax.dot_general(a, b, (((1,), (1,)), ((), ())), preferred_element_type=F32)


def dot_tn(a, b):
    return lax.dot_general(a, b, (((0,), (0,)), ((), ())), preferred_element_type=F32)


def dot_nt_full(a, b):
    return lax.dot_general(
        a, b, (((1,), (1,)), ((), ())), precision=lax.Precision.HIGHEST, preferred_element_type=F32
    )


def peak8(v):
    return jnp.max(jnp.abs(v).reshape(v.shape[0] // 8, 8, v.shape[1]), axis=0)


def at(start, size, step):
    return pl.ds(pl.multiple_of(start, step), size)


def pieces3(v):
    hi = v.astype(BF16)
    rest = v - hi.astype(F32)
    mid = rest.astype(BF16)
    return hi, mid, (rest - mid.astype(F32)).astype(BF16)


def apply_factor(t_t, v):
    hi, mid, low = pieces3(t_t)
    left = jnp.concatenate([hi, hi, hi, mid, mid, low], axis=0)
    hi, mid, low = pieces3(v)
    return dot_tn(left, jnp.concatenate([hi, mid, low, hi, mid, hi], axis=0))


def eliminate(state, first, last):
    row = lax.broadcasted_iota(jnp.int32, (RANK, RANK), 0)
    lane = lax.broadcasted_iota(jnp.int32, (RANK, RANK), 1)

    def step(j, state):
        out = []
        for a, b in state:
            a_row = jnp.sum(jnp.where(row == j, a, 0.0), axis=0, keepdims=True)
            pivot = jnp.sum(jnp.where(lane[:1] == j, a_row, 0.0), axis=1, keepdims=True)
            a_col = jnp.sum(jnp.where(lane == j, a, 0.0), axis=1, keepdims=True)
            b_col = jnp.sum(jnp.where(lane == j, b, 0.0), axis=1, keepdims=True)
            factor = jnp.where(lane[:1] > j, a_row / pivot, 0.0)
            out.append((a - a_col * factor, b - b_col * factor))
        return tuple(out)

    return lax.fori_loop(first, last, step, state)


def identity():
    row = lax.broadcasted_iota(jnp.int32, (RANK, RANK), 0)
    lane = lax.broadcasted_iota(jnp.int32, (RANK, RANK), 1)
    return jnp.where(row == lane, 1.0, 0.0).astype(F32)


def scaled(state):
    eye = identity()
    return [b * (1.0 / jnp.sqrt(jnp.sum(a * eye, axis=0, keepdims=True))) for a, b in state]


def kernel(
    x_hbm, u_hbm, a_hbm, g_hbm, fb_hbm, seed_ref,
    fb, uout,
    xs, gs, ut, ustg, tmp, pdep, pown, tx, rx, q3,
    pt, pc, ps, py, pz, px, pall,
    bt, bc, bs, by, bz, bx, ball, bk4,
    load_x, load_g, load_u, load_fb,
    tx_sem, rx_sem, small_tx, small_rx,
):
    group = lax.axis_index("group")
    rep = lax.axis_index("replica")
    gx = group // SIDE
    gz = group % SIDE
    ry = rep // 2
    rc = rep % 2

    def member(dx, dz):
        return (gx + dx) % SIDE * SIDE + (gz + dz) % SIDE

    def replica(dy, dc):
        return (ry + dy) % SIDE * 2 + (rc + dc) % 2

    def load_step(k, j):
        df, ds = ORDER[j], ORDER[k]
        low = at(ROWS * member(df, ds), 128, 128)
        high = at(ROWS * member(ds, df) + 128, 128, 128)
        for src, dst, sem in ((x_hbm, xs, load_x), (g_hbm, gs, load_g)):
            for part, lanes in enumerate((low, high)):
                pltpu.make_async_copy(
                    src.at[:, lanes], dst.at[k, :, pl.ds(256 * j + 128 * part, 128)], sem.at[4 * k + j]
                ).start()

    load_a = pltpu.make_async_copy(u_hbm.at[:, pl.ds(0, HALF)], ustg, load_u.at[0])
    load_b = pltpu.make_async_copy(
        u_hbm.at[:, pl.ds(HALF, FF - HALF)], ustg.at[:, pl.ds(0, FF - HALF)], load_u.at[1]
    )
    load_c = pltpu.make_async_copy(a_hbm, ustg.at[:, pl.ds(FF - HALF, HD)], load_u.at[2])
    def load_rest():
        for k in range(SIDE):
            for j in range(SIDE):
                if k > 0 or j == SIDE - 1:
                    load_step(k, j)
        pltpu.make_async_copy(fb_hbm, fb, load_fb).start()

    loaded = set()

    def wait_step(k, j):
        if (k, j) in loaded:
            return
        loaded.add((k, j))
        for ref, sem in ((xs, load_x), (gs, load_g)):
            part = ref.at[k, :, pl.ds(256 * j, 256)]
            pltpu.make_async_copy(part, part, sem.at[4 * k + j]).wait()

    barrier = pltpu.get_barrier_semaphore()

    def greet(dy, dc, dx, dz):
        pl.semaphore_signal(
            barrier,
            inc=1,
            device_id={"replica": replica(dy, dc), "group": member(dx, dz)},
            device_id_type=MESH,
        )

    load_a.start()
    load_step(0, 0)
    greet(0, 1, 0, 0)
    for d in range(1, SIDE):
        greet(d, 0, 0, 0)
        greet(1, 0, 0, d)
        greet(SIDE - 1, 0, 0, d)
        greet(0, 0, d, 0)
    greet(0, 0, 0, 1)
    greet(0, 0, 0, SIDE - 1)

    def transpose_u(base, sizes):
        start = 0
        for size in sizes:
            ut[base + start : base + start + size, :] = ustg[:, start : start + size].T
            start += size

    A_TILES = ((0, HALF, xs),)
    B_TILES = ((HALF, FF - HALF, xs), (FF, HD, gs))

    def products(k, lanes, tiles):
        row = 0
        for start, size, source in tiles:
            yield row, size, dot_nn(ut[start : start + size, :], source[k, :, lanes])
            row += size

    def matmul(k, j, tiles, dst, base):
        peak = jnp.zeros((8, ROWS), F32)
        for row, size, value in products(k, slice(256 * j, 256 * j + 256), tiles):
            dst[base + row : base + row + size, :] = value
            peak = jnp.maximum(peak, peak8(value))
        return peak

    def matmul_pair(k, tiles, dst_1, base_1, dst_2, base_2):
        peak = jnp.zeros((8, 2 * ROWS), F32)
        for row, size, value in products(k, slice(256, 768), tiles):
            dst_1[base_1 + row : base_1 + row + size, :] = value[:, :ROWS]
            dst_2[base_2 + row : base_2 + row + size, :] = value[:, ROWS:]
            peak = jnp.maximum(peak, peak8(value))
        return peak[:, :ROWS], peak[:, ROWS:]

    def quantise(src, base, m, slot):
        peak = jnp.maximum(jnp.max(m, axis=0, keepdims=True), 1e-30)
        power = jnp.ceil(jnp.log2(peak))
        scale = jnp.exp2(-power) * LEVELS

        @pl.loop(0, HALF // 64)
        def _(t):
            v = src[at(base + t * 64, 64, 64), :] * scale
            tx[slot, at(t * 64, 64, 64), :] = jnp.round(v).astype(jnp.int32).astype(jnp.int16)

        tx[slot, HALF : HALF + 16, :] = jnp.broadcast_to(power, (16, ROWS)).astype(jnp.int32).astype(jnp.int16)

    def copy_of(slot, mid, kind, stage, h):
        lanes = pl.ds(128 * h, 128)
        along_x = (h == 0) == (stage == 0)
        step = 1 if RIGHTWARD[kind] else SIDE - 1
        peer = member(step, 0) if along_x else member(0, step)
        return pltpu.make_async_remote_copy(
            src_ref=tx.at[slot, :, lanes],
            dst_ref=rx.at[mid, :, lanes],
            send_sem=tx_sem.at[mid, h],
            recv_sem=rx_sem.at[mid, h],
            device_id={"group": peer},
            device_id_type=MESH,
        )

    def slot_of(mid):
        chunk, kind = divmod(mid, 6)
        if chunk == 4:
            return 8 + kind
        return kind + (6 if chunk % 2 and kind < 2 else 0)

    def copies(mid):
        chunk, kind = divmod(mid, 6)
        return [copy_of(slot_of(mid), mid, kind, chunk // 4, h) for h in range(2)]

    pending = {}

    def send(mid, src, base, m, held=()):
        slot = slot_of(mid)
        if slot in pending:
            for c in copies(pending[slot]):
                c.wait_send()
        quantise(src, base, m, slot)
        for h, c in enumerate(copies(mid)):
            if h not in held:
                c.start()
        pending[slot] = mid

    def release(mid, h):
        copies(mid)[h].start()

    def scale_of(mid):
        power = rx[mid, HALF : HALF + 16, :].astype(jnp.int32).astype(F32)[:8]
        return jnp.exp2(power) * (1.0 / LEVELS)

    def combine(acc, base, mids):
        for mid in mids:
            for c in copies(mid):
                c.wait_recv()
        scales = [scale_of(mid) for mid in mids]

        def tile(t, m):
            v = acc[at(base + t * 64, 64, 64), :].reshape(8, 8, ROWS)
            for mid, scale in zip(mids, scales):
                got = rx[mid, at(t * 64, 64, 64), :].astype(jnp.int32).astype(F32).reshape(8, 8, ROWS)
                v = v + got * scale[None]
            acc[at(base + t * 64, 64, 64), :] = v.reshape(64, ROWS)
            return jnp.maximum(m, jnp.max(jnp.abs(v), axis=0))

        return lax.fori_loop(0, HALF // 64, tile, jnp.zeros((8, ROWS), F32))

    def opposite_a(k, held=()):
        wait_step(k, 0)
        m = matmul(k, 0, A_TILES, tmp, 0)
        send(6 * k + OPP_A, tmp, 0, m, held)

    def opposite_b(k):
        wait_step(k, 0)
        m = matmul(k, 0, B_TILES, tmp, 0)
        send(6 * k + OPP_B, tmp, 0, m)

    def pure_b(k, held=()):
        wait_step(k, 1)
        wait_step(k, 2)
        m, _ = matmul_pair(k, B_TILES, tmp, 0, pdep, HALF)
        send(6 * k + PURE_B, tmp, 0, m, held)

    def pure_a(k):
        wait_step(k, 1)
        wait_step(k, 2)
        _, m = matmul_pair(k, A_TILES, pdep, 0, tmp, 0)
        send(6 * k + PURE_A, tmp, 0, m)

    def own(k):
        wait_step(k, 3)
        matmul(k, 3, A_TILES, pown, 0)
        matmul(k, 3, B_TILES, pown, HALF)

    def dependent_a(k):
        m = combine(pdep, 0, [6 * k + OPP_A])
        send(6 * k + DEP_A, pdep, 0, m)

    def dependent_b(k):
        m = combine(pdep, HALF, [6 * k + OPP_B])
        send(6 * k + DEP_B, pdep, HALF, m)

    def complete_a(k):
        more = {0: [], 1: [24 + OPP_A], 2: []}[k]
        m = combine(pown, 0, [6 * k + DEP_A, 6 * k + PURE_A] + more)
        send(24 + (OPP_A, DEP_A, PURE_A)[k], pown, 0, m)

    def complete_b(k):
        more = {0: [], 1: [], 2: [24 + OPP_B]}[k]
        m = combine(pown, HALF, [6 * k + PURE_B, 6 * k + DEP_B] + more)
        send(24 + (OPP_B, PURE_B, DEP_B)[k], pown, HALF, m)

    def finish(base, mids, with_own):
        for mid in mids:
            for c in copies(mid):
                c.wait_recv()
        scales = [scale_of(mid) for mid in mids]
        for t in range(HALF // 128):
            rows = slice(128 * t, 128 * t + 128)
            v = pown[base + 128 * t : base + 128 * t + 128, :].reshape(16, 8, ROWS) if with_own else None
            for mid, scale in zip(mids, scales):
                got = rx[mid, rows, :].astype(jnp.int32).astype(F32).reshape(16, 8, ROWS) * scale[None]
                v = got if v is None else v + got
            columns = slice(base + 128 * t, base + 128 * t + 128)
            fb[:, columns] += v.reshape(128, ROWS).T * (1.0 / GROUP)

    def post(src, dst, which, dy, dc, dx, dz):
        pltpu.make_async_remote_copy(
            src_ref=src,
            dst_ref=dst,
            send_sem=small_tx.at[which],
            recv_sem=small_rx.at[which],
            device_id={"replica": replica(dy, dc), "group": member(dx, dz)},
            device_id_type=MESH,
        ).start()

    def await_bytes(ref, sem):
        pltpu.make_async_copy(ref, ref, sem).wait()

    def all_reduce(src, core, total, chips, zs, xs_, result, first):
        length = src.shape[1]
        quarter = length // SIDE
        core_rows = at(rc * 32, 32, 32)
        my_rows = at(rc * 32 + ry * 8, 8, 8)

        def start():
            post(src.at[at((1 - rc) * 32, 32, 32), :], core, first, 0, 1, 0, 0)

        def along_y():
            await_bytes(core, small_rx.at[first])
            total[...] = src[core_rows, :] + core[...]
            for d in range(1, SIDE):
                post(total.at[at((ry + d) % SIDE * 8, 8, 8), :], chips.at[d - 1], first + 1, d, 0, 0, 0)

        def along_z():
            await_bytes(chips.at[pl.ds(0, 3)], small_rx.at[first + 1])
            chips[3] = (total[at(ry * 8, 8, 8), :] + chips[0]) + (chips[1] + chips[2])
            for d in range(SIDE):
                lanes = at((gz + d) % SIDE * quarter, quarter, 128)
                post(chips.at[3, :, lanes], zs.at[d], first + 2, 1, 0, 0, d)

        def along_x():
            await_bytes(zs.at[pl.ds(0, 4)], small_rx.at[first + 2])
            zs[4] = (zs[0] + zs[1]) + (zs[2] + zs[3])
            for d in range(1, SIDE):
                post(zs.at[4], xs_.at[gx], first + 3, 0, 0, d, 0)
            xs_[gx] = zs[4]

        def back_z():
            await_bytes(xs_.at[pl.ds(0, 3)], small_rx.at[first + 3])
            xs_[4] = (xs_[0] + xs_[1]) + (xs_[2] + xs_[3])
            rows = at(rc * 32 + (ry + SIDE - 1) % SIDE * 8, 8, 8)
            for d in range(SIDE):
                post(
                    xs_.at[4], result.at[rows, at(gz * quarter, quarter, 128)], first + 4, SIDE - 1, 0, 0, d
                )

        def back_y():
            await_bytes(result.at[pl.ds(0, 8), :], small_rx.at[first + 4])
            for d in range(1, SIDE):
                post(result.at[my_rows, :], result.at[my_rows, :], first + 5, d, 0, 0, 0)

        def back_core():
            await_bytes(result.at[pl.ds(0, 24), :], small_rx.at[first + 5])
            post(result.at[core_rows, :], result.at[core_rows, :], first + 6, 0, 1, 0, 0)

        def done():
            await_bytes(result.at[pl.ds(0, 32), :], small_rx.at[first + 6])

        def sent():
            await_bytes(result.at[pl.ds(0, 32), :], small_tx.at[first])
            await_bytes(result.at[pl.ds(0, 24), :], small_tx.at[first + 1])
            await_bytes(result.at[pl.ds(0, 8), :], small_tx.at[first + 2])
            await_bytes(xs_.at[pl.ds(0, 3)], small_tx.at[first + 3])
            await_bytes(result.at[pl.ds(0, 8), :], small_tx.at[first + 4])
            await_bytes(result.at[pl.ds(0, 24), :], small_tx.at[first + 5])
            await_bytes(result.at[pl.ds(0, 32), :], small_tx.at[first + 6])

        return start, along_y, along_z, along_x, back_z, back_y, back_core, done, sent

    def lanes_of(k, j):
        df, ds = ORDER[j], ORDER[k]
        return at(ROWS * member(df, ds), 128, 128), at(ROWS * member(ds, df) + 128, 128, 128)

    def make_factors():
        seed = seed_ref[0]
        for t in range(9):
            layer = t // 7
            q = factor_t(seed, 256 * (t - 7 * layer), 256, layer)
            q3[:, 256 * t : 256 * t + 256] = split3(q)

    def project():
        w_l = split3(fold3(dot_nn(q3[:, :FF], ut[:FF, :])))
        w_r = split3(fold3(dot_nn(q3[:, FF:], ut[FF:, :])))
        for k in range(SIDE):
            p_l = fold3(dot_nn(w_l, xs[k])) * (1.0 / 128)
            p_r = fold3(dot_nn(w_r, gs[k])) * (1.0 / 128)
            for j in range(SIDE):
                for part, lanes in enumerate(lanes_of(k, j)):
                    here = slice(256 * j + 128 * part, 256 * j + 128 * part + 128)
                    pt[:RANK, lanes] = p_l[:, here]
                    pt[RANK:, lanes] = p_r[:, here]

        mine = at(ROWS * group, ROWS, 128)
        for rows, columns in ((slice(0, RANK), slice(0, FF)), (slice(RANK, 64), slice(FF, W))):
            hi, low = split2(fb[:, columns])
            term = fold3(dot_nt(q3[:, columns], hi)) + fold3(dot_nt(q3[:, columns], low))
            pt[rows, mine] += term * (1.0 / 8)

    def back_project():
        y_l = jnp.zeros((96, TOK), F32)
        y_r = jnp.zeros((96, TOK), F32)
        for k in range(SIDE):
            parts = []
            for j in range(SIDE):
                for lanes in lanes_of(k, j):
                    parts.append(pall[:, lanes])
            p = jnp.concatenate(parts, axis=1)
            y_l = y_l + dot_nt(split3(p[:RANK]), xs[k])
            y_r = y_r + dot_nt(split3(p[RANK:]), gs[k])
        y_l = split3(fold3(y_l) * (1.0 / 128))
        y_r = split3(fold3(y_r) * (1.0 / 128))
        p = pall[:, at(ROWS * group, ROWS, 128)] * (1.0 / 8)
        p_l, p_r = split3(p[:RANK]), split3(p[RANK:])

        def piece(y, p3, columns):
            hi, low = split2(fb[:, columns])
            return fold3(dot_nt(y, ut[columns, :])) + (fold3(dot_nn(p3, hi)) + fold3(dot_nn(p3, low)))

        bt[:RANK, :HALF] = piece(y_l, p_l, slice(0, HALF))
        bt[RANK:, 0:640] = piece(y_l, p_l, slice(HALF, FF))
        bt[RANK:, 640:HALF] = piece(y_r, p_r, slice(FF, W))
        bt[:, HALF:] = jnp.zeros((64, BLEN - HALF), F32)

    def grams():
        eye = identity()
        return tuple(
            (dot_nt_full(pall[rows, :], pall[rows, :]), eye) for rows in (slice(0, RANK), slice(RANK, 64))
        )

    def quad(v, last):
        hi, low = split2(v)
        return jnp.concatenate([hi, hi, low, low] if last else [hi, low, hi, low], axis=0)

    def bases(t_l, t_r, lanes):
        return jnp.concatenate(
            [
                quad(apply_factor(t_l, pall[:RANK, lanes]), True),
                quad(apply_factor(t_r, pall[RANK:, lanes]), True),
            ],
            axis=0,
        )

    def decompress(t_l, t_r):
        mine = bases(t_l, t_r, at(ROWS * group, ROWS, 128)).T
        pieces = (
            (t_l, slice(0, RANK), 0, HALF, 0),
            (t_l, slice(RANK, 64), 0, 640, HALF),
            (t_r, slice(RANK, 64), 640, HALF, HALF),
        )
        for t, rows, lo, hi, base in pieces:
            b4 = quad(apply_factor(t, ball[rows, lo:hi]), False)
            none = jnp.zeros_like(b4)
            left = base + lo < FF
            both = jnp.concatenate([b4, none] if left else [none, b4], axis=0)
            fb[:, base + lo : base + hi] -= dot_nn(mine, both)
            bk4[base + lo : base + hi, :] = both.T

    def decompress_update(t_l, t_r):
        width = W // REP
        chosen = bk4[at(rep * width, width, 16), :]
        for t in range(4):
            lanes = slice(1024 * t, 1024 * t + 1024)
            uout[:, lanes] = dot_nn(chosen, bases(t_l, t_r, lanes)).astype(BF16)

    p_steps = all_reduce(pt, pc, ps, py, pz, px, pall, 0)
    b_steps = all_reduce(bt, bc, bs, by, bz, bx, ball, 7)

    load_step(0, 1)
    load_step(0, 2)
    load_a.wait()
    transpose_u(0, (384, 384, 384))
    load_b.start()
    load_c.start()
    pl.semaphore_wait(barrier, 15)
    opposite_a(0)
    load_b.wait()
    load_c.wait()
    transpose_u(HALF, (256, 384, 256, 256))
    load_rest()
    opposite_b(0)
    pure_b(0)
    pure_a(0)
    make_factors()
    for k in range(SIDE):
        for j in range(SIDE):
            wait_step(k, j)
    pltpu.make_async_copy(fb_hbm, fb, load_fb).wait()
    project()
    p_steps[0]()
    own(0)
    p_steps[1]()
    opposite_a(1)
    opposite_b(1)
    dependent_a(0)
    dependent_b(0)
    pure_b(1)
    pure_a(1)
    p_steps[2]()
    p_steps[3]()
    dependent_a(1)
    dependent_b(1)
    complete_a(0)
    complete_b(0)
    opposite_a(2)
    opposite_b(2)
    own(1)
    p_steps[4]()
    pure_b(2)
    pure_a(2)
    p_steps[5]()
    dependent_a(2)
    dependent_b(2)
    p_steps[6]()
    complete_a(1)
    complete_b(1)
    p_steps[7]()
    back_project()
    b_steps[0]()
    opposite_b(3)
    opposite_a(3, held=(0,))
    b_steps[1]()
    own(2)
    pure_a(3)
    pure_b(3, held=(0,))
    state = eliminate(grams(), 0, 8)
    b_steps[2]()
    state = eliminate(state, 8, 20)
    b_steps[3]()
    release(18 + OPP_A, 0)
    release(18 + PURE_B, 0)
    complete_b(2)
    complete_a(2)
    state = eliminate(state, 20, RANK)
    t_l, t_r = scaled(state)
    b_steps[4]()
    own(3)
    dependent_b(3)
    b_steps[5]()
    b_steps[6]()
    dependent_a(3)
    finish(0, [18 + PURE_A, 24 + DEP_A, 24 + PURE_A], True)
    finish(HALF, [18 + PURE_B, 24 + PURE_B, 24 + DEP_B], True)
    b_steps[7]()
    decompress(t_l, t_r)
    decompress_update(t_l, t_r)
    finish(HALF, [18 + DEP_B], False)
    finish(0, [18 + DEP_A], False)

    for slot in pending:
        for c in copies(pending[slot]):
            c.wait_send()
    p_steps[8]()
    b_steps[8]()


def small_buffers(length):
    quarter = length // SIDE
    shapes = (
        (64, length), (32, length), (32, length), (4, 8, length), (5, 8, quarter), (5, 8, quarter), (64, length)
    )
    return [pltpu.VMEM(shape, F32) for shape in shapes]


def on_device(layer_input, up_cotangent, attn_values, resid_cotangent, feedback, start_seed):
    hbm = pl.BlockSpec(memory_space=pl.ANY)
    vmem = pl.BlockSpec(memory_space=pltpu.VMEM)
    dma = pltpu.SemaphoreType.DMA
    new_feedback, update = pl.pallas_call(
        kernel,
        out_shape=(
            pltpu.VMEM((ROWS, W), F32),
            pltpu.VMEM((W // REP, D), BF16),
        ),
        in_specs=[hbm] * 5 + [pl.BlockSpec(memory_space=pltpu.SMEM)],
        out_specs=(vmem, vmem),
        scratch_shapes=[
            pltpu.VMEM((SIDE, TOK, SIDE * ROWS), BF16),
            pltpu.VMEM((SIDE, TOK, SIDE * ROWS), BF16),
            pltpu.VMEM((W, TOK), BF16),
            pltpu.VMEM((TOK, HALF), BF16),
            pltpu.VMEM((HALF, ROWS), F32),
            pltpu.VMEM((W, ROWS), F32),
            pltpu.VMEM((W, ROWS), F32),
            pltpu.VMEM((14, HALF + 16, ROWS), jnp.int16),
            pltpu.VMEM((30, HALF + 16, ROWS), jnp.int16),
            pltpu.VMEM((96, W), BF16),
            *small_buffers(D),
            *small_buffers(BLEN),
            pltpu.VMEM((W, 256), BF16),
            dma((GROUP,)),
            dma((GROUP,)),
            dma((3,)),
            dma,
            dma((30, 2)),
            dma((30, 2)),
            dma((14,)),
            dma((14,)),
        ],
        compiler_params=pltpu.CompilerParams(
            collective_id=0, has_side_effects=True, vmem_limit_bytes=58 * 1024 * 1024
        ),
        cost_estimate=pl.CostEstimate(flops=2 * TOK * D * W, bytes_accessed=21_000_000, transcendentals=0),
    )(layer_input, up_cotangent, attn_values, resid_cotangent, feedback[0], start_seed)
    return (update.T, new_feedback[None])


def solution(mesh):
    in_specs = (
        P(("replica", "group"), None),
        P(("replica", "group"), None),
        P(("replica", "group"), None),
        P(("replica", "group"), None),
        P("replica", "group", None),
        P(),
    )
    out_specs = (P(None, "replica"), P("replica", "group", None))
    return jax.shard_map(
        on_device, mesh=mesh, in_specs=in_specs, out_specs=out_specs, check_vma=False
    )
```

```python
import jax
import jax.numpy as jnp
from jax import lax
from jax.experimental import pallas as pl
from jax.experimental.pallas import tpu as pltpu
from jax.sharding import PartitionSpec as P

RANK = 32
TOK = 768
D = 4096
FF = 1792
HD = 512
W = FF + HD
HALF = W // 2
ROWS = 256
SIDE = 4
GROUP = 16
REP = 8
BLEN = 1536
LEVELS = 32700.0
ORDER = (2, 1, 3, 0)
MESH = pl.DeviceIdType.MESH
F32 = jnp.float32
BF16 = jnp.bfloat16
OPP_A, OPP_B, PURE_B, PURE_A, DEP_A, DEP_B = range(6)
RIGHTWARD = (True, False, True, False, True, False)


def modulo(v):
    r = v - jnp.floor(v * (1.0 / 65521.0)) * 65521.0
    r = jnp.where(r < 0.0, r + 65521.0, r)
    return jnp.where(r >= 65521.0, r - 65521.0, r)


def factor_t(seed, first, count, layer):
    positions = lax.broadcasted_iota(jnp.int32, (RANK, count), 1) + first
    columns = lax.broadcasted_iota(jnp.int32, (RANK, count), 0)
    base = (seed % 65521) * 31 + layer * 4099 + 12345
    mixed = modulo((base + positions * 977 + columns * 7919).astype(F32)).astype(jnp.int32)
    folded = (mixed & 255) * (mixed >> 8)
    final = modulo((folded * 181 + mixed).astype(F32))
    return (final / 65521.0 - 0.5) * 3.4


def split3(v):
    hi = v.astype(BF16)
    rest = v - hi.astype(F32)
    mid = rest.astype(BF16)
    low = (rest - mid.astype(F32)).astype(BF16)
    return jnp.concatenate([hi, mid, low], axis=0)


def split2(v):
    hi = v.astype(BF16)
    return hi, (v - hi.astype(F32)).astype(BF16)


def fold3(v):
    return (v[64:96] + v[32:64]) + v[0:32]


def dot_nn(a, b):
    return lax.dot_general(a, b, (((1,), (0,)), ((), ())), preferred_element_type=F32)


def dot_nt(a, b):
    return lax.dot_general(a, b, (((1,), (1,)), ((), ())), preferred_element_type=F32)


def dot_tn(a, b):
    return lax.dot_general(a, b, (((0,), (0,)), ((), ())), preferred_element_type=F32)


def dot_nt_full(a, b):
    return lax.dot_general(
        a, b, (((1,), (1,)), ((), ())), precision=lax.Precision.HIGHEST, preferred_element_type=F32
    )


def peak8(v):
    return jnp.max(jnp.abs(v).reshape(v.shape[0] // 8, 8, v.shape[1]), axis=0)


def at(start, size, step):
    return pl.ds(pl.multiple_of(start, step), size)


def pieces3(v):
    hi = v.astype(BF16)
    rest = v - hi.astype(F32)
    mid = rest.astype(BF16)
    return hi, mid, (rest - mid.astype(F32)).astype(BF16)


def apply_factor(t_t, v):
    hi, mid, low = pieces3(t_t)
    left = jnp.concatenate([hi, hi, hi, mid, mid, low], axis=0)
    hi, mid, low = pieces3(v)
    return dot_tn(left, jnp.concatenate([hi, mid, low, hi, mid, hi], axis=0))


def eliminate(state, first, last):
    row = lax.broadcasted_iota(jnp.int32, (RANK, RANK), 0)
    lane = lax.broadcasted_iota(jnp.int32, (RANK, RANK), 1)

    def step(j, state):
        out = []
        for a, b in state:
            a_row = jnp.sum(jnp.where(row == j, a, 0.0), axis=0, keepdims=True)
            pivot = jnp.sum(jnp.where(lane[:1] == j, a_row, 0.0), axis=1, keepdims=True)
            a_col = jnp.sum(jnp.where(lane == j, a, 0.0), axis=1, keepdims=True)
            b_col = jnp.sum(jnp.where(lane == j, b, 0.0), axis=1, keepdims=True)
            factor = jnp.where(lane[:1] > j, a_row / pivot, 0.0)
            out.append((a - a_col * factor, b - b_col * factor))
        return tuple(out)

    return lax.fori_loop(first, last, step, state)


def identity():
    row = lax.broadcasted_iota(jnp.int32, (RANK, RANK), 0)
    lane = lax.broadcasted_iota(jnp.int32, (RANK, RANK), 1)
    return jnp.where(row == lane, 1.0, 0.0).astype(F32)


def scaled(state):
    eye = identity()
    return [b * (1.0 / jnp.sqrt(jnp.sum(a * eye, axis=0, keepdims=True))) for a, b in state]


def kernel(
    x_hbm, u_hbm, a_hbm, g_hbm, fb_hbm, seed_ref,
    fb, uout,
    xs, gs, ut, ustg, tmp, pdep, pown, tx, rx, q3,
    pt, pc, ps, py, pz, px, pall,
    bt, bc, bs, by, bz, bx, ball, bk4,
    load_x, load_g, load_u, load_fb,
    tx_sem, rx_sem, small_tx, small_rx,
):
    group = lax.axis_index("group")
    rep = lax.axis_index("replica")
    gx = group // SIDE
    gz = group % SIDE
    ry = rep // 2
    rc = rep % 2

    def member(dx, dz):
        return (gx + dx) % SIDE * SIDE + (gz + dz) % SIDE

    def replica(dy, dc):
        return (ry + dy) % SIDE * 2 + (rc + dc) % 2

    def load_step(k, j):
        df, ds = ORDER[j], ORDER[k]
        low = at(ROWS * member(df, ds), 128, 128)
        high = at(ROWS * member(ds, df) + 128, 128, 128)
        for src, dst, sem in ((x_hbm, xs, load_x), (g_hbm, gs, load_g)):
            for part, lanes in enumerate((low, high)):
                pltpu.make_async_copy(
                    src.at[:, lanes], dst.at[k, :, pl.ds(256 * j + 128 * part, 128)], sem.at[4 * k + j]
                ).start()

    load_a = pltpu.make_async_copy(u_hbm.at[:, pl.ds(0, HALF)], ustg, load_u.at[0])
    load_b = pltpu.make_async_copy(
        u_hbm.at[:, pl.ds(HALF, FF - HALF)], ustg.at[:, pl.ds(0, FF - HALF)], load_u.at[1]
    )
    load_c = pltpu.make_async_copy(a_hbm, ustg.at[:, pl.ds(FF - HALF, HD)], load_u.at[2])
    def load_rest():
        for k in range(SIDE):
            for j in range(SIDE):
                if k > 0 or j == SIDE - 1:
                    load_step(k, j)
        pltpu.make_async_copy(fb_hbm, fb, load_fb).start()

    loaded = set()

    def wait_step(k, j):
        if (k, j) in loaded:
            return
        loaded.add((k, j))
        for ref, sem in ((xs, load_x), (gs, load_g)):
            part = ref.at[k, :, pl.ds(256 * j, 256)]
            pltpu.make_async_copy(part, part, sem.at[4 * k + j]).wait()

    barrier = pltpu.get_barrier_semaphore()

    def greet(dy, dc, dx, dz):
        pl.semaphore_signal(
            barrier,
            inc=1,
            device_id={"replica": replica(dy, dc), "group": member(dx, dz)},
            device_id_type=MESH,
        )

    load_a.start()
    load_step(0, 0)
    greet(0, 1, 0, 0)
    for d in range(1, SIDE):
        greet(d, 0, 0, 0)
        greet(1, 0, 0, d)
        greet(SIDE - 1, 0, 0, d)
        greet(0, 0, d, 0)
    greet(0, 0, 0, 1)
    greet(0, 0, 0, SIDE - 1)

    def transpose_u(base, sizes):
        start = 0
        for size in sizes:
            ut[base + start : base + start + size, :] = ustg[:, start : start + size].T
            start += size

    A_TILES = ((0, HALF, xs),)
    B_TILES = ((HALF, FF - HALF, xs), (FF, HD, gs))

    def products(k, lanes, tiles):
        row = 0
        for start, size, source in tiles:
            yield row, size, dot_nn(ut[start : start + size, :], source[k, :, lanes])
            row += size

    def matmul(k, j, tiles, dst, base):
        peak = jnp.zeros((8, ROWS), F32)
        for row, size, value in products(k, slice(256 * j, 256 * j + 256), tiles):
            dst[base + row : base + row + size, :] = value
            peak = jnp.maximum(peak, peak8(value))
        return peak

    def matmul_pair(k, tiles, dst_1, base_1, dst_2, base_2):
        peak = jnp.zeros((8, 2 * ROWS), F32)
        for row, size, value in products(k, slice(256, 768), tiles):
            dst_1[base_1 + row : base_1 + row + size, :] = value[:, :ROWS]
            dst_2[base_2 + row : base_2 + row + size, :] = value[:, ROWS:]
            peak = jnp.maximum(peak, peak8(value))
        return peak[:, :ROWS], peak[:, ROWS:]

    def quantise(src, base, m, slot):
        peak = jnp.maximum(jnp.max(m, axis=0, keepdims=True), 1e-30)
        power = jnp.ceil(jnp.log2(peak))
        scale = jnp.exp2(-power) * LEVELS

        @pl.loop(0, HALF // 64)
        def _(t):
            v = src[at(base + t * 64, 64, 64), :] * scale
            tx[slot, at(t * 64, 64, 64), :] = jnp.round(v).astype(jnp.int32).astype(jnp.int16)

        tx[slot, HALF : HALF + 16, :] = jnp.broadcast_to(power, (16, ROWS)).astype(jnp.int32).astype(jnp.int16)

    def copy_of(slot, mid, kind, stage, h):
        lanes = pl.ds(128 * h, 128)
        along_x = (h == 0) == (stage == 0)
        step = 1 if RIGHTWARD[kind] else SIDE - 1
        peer = member(step, 0) if along_x else member(0, step)
        return pltpu.make_async_remote_copy(
            src_ref=tx.at[slot, :, lanes],
            dst_ref=rx.at[mid, :, lanes],
            send_sem=tx_sem.at[mid, h],
            recv_sem=rx_sem.at[mid, h],
            device_id={"group": peer},
            device_id_type=MESH,
        )

    def slot_of(mid):
        chunk, kind = divmod(mid, 6)
        if chunk == 4:
            return 8 + kind
        return kind + (6 if chunk % 2 and kind < 2 else 0)

    def copies(mid):
        chunk, kind = divmod(mid, 6)
        return [copy_of(slot_of(mid), mid, kind, chunk // 4, h) for h in range(2)]

    pending = {}

    def send(mid, src, base, m, held=()):
        slot = slot_of(mid)
        if slot in pending:
            for c in copies(pending[slot]):
                c.wait_send()
        quantise(src, base, m, slot)
        for h, c in enumerate(copies(mid)):
            if h not in held:
                c.start()
        pending[slot] = mid

    def release(mid, h):
        copies(mid)[h].start()

    def scale_of(mid):
        power = rx[mid, HALF : HALF + 16, :].astype(jnp.int32).astype(F32)[:8]
        return jnp.exp2(power) * (1.0 / LEVELS)

    def combine(acc, base, mids):
        for mid in mids:
            for c in copies(mid):
                c.wait_recv()
        scales = [scale_of(mid) for mid in mids]

        def tile(t, m):
            v = acc[at(base + t * 64, 64, 64), :].reshape(8, 8, ROWS)
            for mid, scale in zip(mids, scales):
                got = rx[mid, at(t * 64, 64, 64), :].astype(jnp.int32).astype(F32).reshape(8, 8, ROWS)
                v = v + got * scale[None]
            acc[at(base + t * 64, 64, 64), :] = v.reshape(64, ROWS)
            return jnp.maximum(m, jnp.max(jnp.abs(v), axis=0))

        return lax.fori_loop(0, HALF // 64, tile, jnp.zeros((8, ROWS), F32))

    def opposite_a(k, held=()):
        wait_step(k, 0)
        m = matmul(k, 0, A_TILES, tmp, 0)
        send(6 * k + OPP_A, tmp, 0, m, held)

    def opposite_b(k):
        wait_step(k, 0)
        m = matmul(k, 0, B_TILES, tmp, 0)
        send(6 * k + OPP_B, tmp, 0, m)

    def pure_b(k, held=()):
        wait_step(k, 1)
        wait_step(k, 2)
        m, _ = matmul_pair(k, B_TILES, tmp, 0, pdep, HALF)
        send(6 * k + PURE_B, tmp, 0, m, held)

    def pure_a(k):
        wait_step(k, 1)
        wait_step(k, 2)
        _, m = matmul_pair(k, A_TILES, pdep, 0, tmp, 0)
        send(6 * k + PURE_A, tmp, 0, m)

    def own(k):
        wait_step(k, 3)
        matmul(k, 3, A_TILES, pown, 0)
        matmul(k, 3, B_TILES, pown, HALF)

    def dependent_a(k):
        m = combine(pdep, 0, [6 * k + OPP_A])
        send(6 * k + DEP_A, pdep, 0, m)

    def dependent_b(k):
        m = combine(pdep, HALF, [6 * k + OPP_B])
        send(6 * k + DEP_B, pdep, HALF, m)

    def complete_a(k):
        more = {0: [], 1: [24 + OPP_A], 2: []}[k]
        m = combine(pown, 0, [6 * k + DEP_A, 6 * k + PURE_A] + more)
        send(24 + (OPP_A, DEP_A, PURE_A)[k], pown, 0, m)

    def complete_b(k):
        more = {0: [], 1: [], 2: [24 + OPP_B]}[k]
        m = combine(pown, HALF, [6 * k + PURE_B, 6 * k + DEP_B] + more)
        send(24 + (OPP_B, PURE_B, DEP_B)[k], pown, HALF, m)

    def finish(base, mids, with_own):
        for mid in mids:
            for c in copies(mid):
                c.wait_recv()
        scales = [scale_of(mid) for mid in mids]
        for t in range(HALF // 128):
            rows = slice(128 * t, 128 * t + 128)
            v = pown[base + 128 * t : base + 128 * t + 128, :].reshape(16, 8, ROWS) if with_own else None
            for mid, scale in zip(mids, scales):
                got = rx[mid, rows, :].astype(jnp.int32).astype(F32).reshape(16, 8, ROWS) * scale[None]
                v = got if v is None else v + got
            columns = slice(base + 128 * t, base + 128 * t + 128)
            fb[:, columns] += v.reshape(128, ROWS).T * (1.0 / GROUP)

    def post(src, dst, which, dy, dc, dx, dz):
        pltpu.make_async_remote_copy(
            src_ref=src,
            dst_ref=dst,
            send_sem=small_tx.at[which],
            recv_sem=small_rx.at[which],
            device_id={"replica": replica(dy, dc), "group": member(dx, dz)},
            device_id_type=MESH,
        ).start()

    def await_bytes(ref, sem):
        pltpu.make_async_copy(ref, ref, sem).wait()

    def all_reduce(src, core, total, chips, zs, xs_, result, first):
        length = src.shape[1]
        quarter = length // SIDE
        core_rows = at(rc * 32, 32, 32)
        my_rows = at(rc * 32 + ry * 8, 8, 8)

        def start():
            post(src.at[at((1 - rc) * 32, 32, 32), :], core, first, 0, 1, 0, 0)

        def along_y():
            await_bytes(core, small_rx.at[first])
            total[...] = src[core_rows, :] + core[...]
            for d in range(1, SIDE):
                post(total.at[at((ry + d) % SIDE * 8, 8, 8), :], chips.at[d - 1], first + 1, d, 0, 0, 0)

        def along_z():
            await_bytes(chips.at[pl.ds(0, 3)], small_rx.at[first + 1])
            chips[3] = (total[at(ry * 8, 8, 8), :] + chips[0]) + (chips[1] + chips[2])
            for d in range(SIDE):
                lanes = at((gz + d) % SIDE * quarter, quarter, 128)
                post(chips.at[3, :, lanes], zs.at[d], first + 2, 1, 0, 0, d)

        def along_x():
            await_bytes(zs.at[pl.ds(0, 4)], small_rx.at[first + 2])
            zs[4] = (zs[0] + zs[1]) + (zs[2] + zs[3])
            for d in range(1, SIDE):
                post(zs.at[4], xs_.at[gx], first + 3, 0, 0, d, 0)
            xs_[gx] = zs[4]

        def back_z():
            await_bytes(xs_.at[pl.ds(0, 3)], small_rx.at[first + 3])
            xs_[4] = (xs_[0] + xs_[1]) + (xs_[2] + xs_[3])
            rows = at(rc * 32 + (ry + SIDE - 1) % SIDE * 8, 8, 8)
            for d in range(SIDE):
                post(
                    xs_.at[4], result.at[rows, at(gz * quarter, quarter, 128)], first + 4, SIDE - 1, 0, 0, d
                )

        def back_y():
            await_bytes(result.at[pl.ds(0, 8), :], small_rx.at[first + 4])
            for d in range(1, SIDE):
                post(result.at[my_rows, :], result.at[my_rows, :], first + 5, d, 0, 0, 0)

        def back_core():
            await_bytes(result.at[pl.ds(0, 24), :], small_rx.at[first + 5])
            post(result.at[core_rows, :], result.at[core_rows, :], first + 6, 0, 1, 0, 0)

        def done():
            await_bytes(result.at[pl.ds(0, 32), :], small_rx.at[first + 6])

        def sent():
            await_bytes(result.at[pl.ds(0, 32), :], small_tx.at[first])
            await_bytes(result.at[pl.ds(0, 24), :], small_tx.at[first + 1])
            await_bytes(result.at[pl.ds(0, 8), :], small_tx.at[first + 2])
            await_bytes(xs_.at[pl.ds(0, 3)], small_tx.at[first + 3])
            await_bytes(result.at[pl.ds(0, 8), :], small_tx.at[first + 4])
            await_bytes(result.at[pl.ds(0, 24), :], small_tx.at[first + 5])
            await_bytes(result.at[pl.ds(0, 32), :], small_tx.at[first + 6])

        return start, along_y, along_z, along_x, back_z, back_y, back_core, done, sent

    def lanes_of(k, j):
        df, ds = ORDER[j], ORDER[k]
        return at(ROWS * member(df, ds), 128, 128), at(ROWS * member(ds, df) + 128, 128, 128)

    def make_factors():
        seed = seed_ref[0]
        for t in range(9):
            layer = t // 7
            q = factor_t(seed, 256 * (t - 7 * layer), 256, layer)
            q3[:, 256 * t : 256 * t + 256] = split3(q)

    def project():
        w_l = split3(fold3(dot_nn(q3[:, :FF], ut[:FF, :])))
        w_r = split3(fold3(dot_nn(q3[:, FF:], ut[FF:, :])))
        for k in range(SIDE):
            p_l = fold3(dot_nn(w_l, xs[k])) * (1.0 / 128)
            p_r = fold3(dot_nn(w_r, gs[k])) * (1.0 / 128)
            for j in range(SIDE):
                for part, lanes in enumerate(lanes_of(k, j)):
                    here = slice(256 * j + 128 * part, 256 * j + 128 * part + 128)
                    pt[:RANK, lanes] = p_l[:, here]
                    pt[RANK:, lanes] = p_r[:, here]

        mine = at(ROWS * group, ROWS, 128)
        for rows, columns in ((slice(0, RANK), slice(0, FF)), (slice(RANK, 64), slice(FF, W))):
            hi, low = split2(fb[:, columns])
            term = fold3(dot_nt(q3[:, columns], hi)) + fold3(dot_nt(q3[:, columns], low))
            pt[rows, mine] += term * (1.0 / 8)

    def back_project():
        y_l = jnp.zeros((96, TOK), F32)
        y_r = jnp.zeros((96, TOK), F32)
        for k in range(SIDE):
            parts = []
            for j in range(SIDE):
                for lanes in lanes_of(k, j):
                    parts.append(pall[:, lanes])
            p = jnp.concatenate(parts, axis=1)
            y_l = y_l + dot_nt(split3(p[:RANK]), xs[k])
            y_r = y_r + dot_nt(split3(p[RANK:]), gs[k])
        y_l = split3(fold3(y_l) * (1.0 / 128))
        y_r = split3(fold3(y_r) * (1.0 / 128))
        p = pall[:, at(ROWS * group, ROWS, 128)] * (1.0 / 8)
        p_l, p_r = split3(p[:RANK]), split3(p[RANK:])

        def piece(y, p3, columns):
            hi, low = split2(fb[:, columns])
            return fold3(dot_nt(y, ut[columns, :])) + (fold3(dot_nn(p3, hi)) + fold3(dot_nn(p3, low)))

        bt[:RANK, :HALF] = piece(y_l, p_l, slice(0, HALF))
        bt[RANK:, 0:640] = piece(y_l, p_l, slice(HALF, FF))
        bt[RANK:, 640:HALF] = piece(y_r, p_r, slice(FF, W))
        bt[:, HALF:] = jnp.zeros((64, BLEN - HALF), F32)

    def grams():
        eye = identity()
        return tuple(
            (dot_nt_full(pall[rows, :], pall[rows, :]), eye) for rows in (slice(0, RANK), slice(RANK, 64))
        )

    def quad(v, last):
        hi, low = split2(v)
        return jnp.concatenate([hi, hi, low, low] if last else [hi, low, hi, low], axis=0)

    def bases(t_l, t_r, lanes):
        return jnp.concatenate(
            [
                quad(apply_factor(t_l, pall[:RANK, lanes]), True),
                quad(apply_factor(t_r, pall[RANK:, lanes]), True),
            ],
            axis=0,
        )

    def decompress(t_l, t_r):
        mine = bases(t_l, t_r, at(ROWS * group, ROWS, 128)).T
        pieces = (
            (t_l, slice(0, RANK), 0, HALF, 0),
            (t_l, slice(RANK, 64), 0, 640, HALF),
            (t_r, slice(RANK, 64), 640, HALF, HALF),
        )
        for t, rows, lo, hi, base in pieces:
            b4 = quad(apply_factor(t, ball[rows, lo:hi]), False)
            none = jnp.zeros_like(b4)
            left = base + lo < FF
            both = jnp.concatenate([b4, none] if left else [none, b4], axis=0)
            fb[:, base + lo : base + hi] -= dot_nn(mine, both)
            bk4[base + lo : base + hi, :] = both.T

    def decompress_update(t_l, t_r):
        width = W // REP
        chosen = bk4[at(rep * width, width, 16), :]
        for t in range(4):
            lanes = slice(1024 * t, 1024 * t + 1024)
            uout[:, lanes] = dot_nn(chosen, bases(t_l, t_r, lanes)).astype(BF16)

    p_steps = all_reduce(pt, pc, ps, py, pz, px, pall, 0)
    b_steps = all_reduce(bt, bc, bs, by, bz, bx, ball, 7)

    load_step(0, 1)
    load_step(0, 2)
    load_a.wait()
    transpose_u(0, (384, 384, 384))
    load_b.start()
    load_c.start()
    pl.semaphore_wait(barrier, 15)
    opposite_a(0)
    load_b.wait()
    load_c.wait()
    transpose_u(HALF, (256, 384, 256, 256))
    load_rest()
    opposite_b(0)
    pure_b(0)
    pure_a(0)
    make_factors()
    opposite_b(1)
    for k in range(SIDE):
        for j in range(SIDE):
            wait_step(k, j)
    pltpu.make_async_copy(fb_hbm, fb, load_fb).wait()
    project()
    p_steps[0]()
    opposite_a(1)
    dependent_a(0)
    p_steps[1]()
    dependent_b(0)
    own(0)
    pure_b(1)
    pure_a(1)
    p_steps[2]()
    p_steps[3]()
    dependent_a(1)
    dependent_b(1)
    complete_a(0)
    complete_b(0)
    opposite_a(2)
    opposite_b(2)
    own(1)
    p_steps[4]()
    pure_b(2)
    pure_a(2)
    p_steps[5]()
    dependent_a(2)
    dependent_b(2)
    p_steps[6]()
    complete_a(1)
    complete_b(1)
    p_steps[7]()
    back_project()
    b_steps[0]()
    opposite_b(3)
    opposite_a(3, held=(0,))
    b_steps[1]()
    own(2)
    pure_a(3)
    pure_b(3, held=(0,))
    state = eliminate(grams(), 0, 8)
    b_steps[2]()
    state = eliminate(state, 8, 20)
    b_steps[3]()
    release(18 + OPP_A, 0)
    release(18 + PURE_B, 0)
    complete_b(2)
    complete_a(2)
    state = eliminate(state, 20, RANK)
    t_l, t_r = scaled(state)
    b_steps[4]()
    own(3)
    dependent_b(3)
    b_steps[5]()
    dependent_a(3)
    b_steps[6]()
    finish(0, [18 + PURE_A, 24 + DEP_A, 24 + PURE_A], True)
    finish(HALF, [18 + PURE_B, 24 + PURE_B, 24 + DEP_B], True)
    b_steps[7]()
    decompress(t_l, t_r)
    decompress_update(t_l, t_r)
    finish(HALF, [18 + DEP_B], False)
    finish(0, [18 + DEP_A], False)

    for slot in pending:
        for c in copies(pending[slot]):
            c.wait_send()
    p_steps[8]()
    b_steps[8]()


def small_buffers(length):
    quarter = length // SIDE
    shapes = (
        (64, length), (32, length), (32, length), (4, 8, length), (5, 8, quarter), (5, 8, quarter), (64, length)
    )
    return [pltpu.VMEM(shape, F32) for shape in shapes]


def on_device(layer_input, up_cotangent, attn_values, resid_cotangent, feedback, start_seed):
    hbm = pl.BlockSpec(memory_space=pl.ANY)
    vmem = pl.BlockSpec(memory_space=pltpu.VMEM)
    dma = pltpu.SemaphoreType.DMA
    new_feedback, update = pl.pallas_call(
        kernel,
        out_shape=(
            pltpu.VMEM((ROWS, W), F32),
            pltpu.VMEM((W // REP, D), BF16),
        ),
        in_specs=[hbm] * 5 + [pl.BlockSpec(memory_space=pltpu.SMEM)],
        out_specs=(vmem, vmem),
        scratch_shapes=[
            pltpu.VMEM((SIDE, TOK, SIDE * ROWS), BF16),
            pltpu.VMEM((SIDE, TOK, SIDE * ROWS), BF16),
            pltpu.VMEM((W, TOK), BF16),
            pltpu.VMEM((TOK, HALF), BF16),
            pltpu.VMEM((HALF, ROWS), F32),
            pltpu.VMEM((W, ROWS), F32),
            pltpu.VMEM((W, ROWS), F32),
            pltpu.VMEM((14, HALF + 16, ROWS), jnp.int16),
            pltpu.VMEM((30, HALF + 16, ROWS), jnp.int16),
            pltpu.VMEM((96, W), BF16),
            *small_buffers(D),
            *small_buffers(BLEN),
            pltpu.VMEM((W, 256), BF16),
            dma((GROUP,)),
            dma((GROUP,)),
            dma((3,)),
            dma,
            dma((30, 2)),
            dma((30, 2)),
            dma((14,)),
            dma((14,)),
        ],
        compiler_params=pltpu.CompilerParams(
            collective_id=0, has_side_effects=True, vmem_limit_bytes=58 * 1024 * 1024
        ),
        cost_estimate=pl.CostEstimate(flops=2 * TOK * D * W, bytes_accessed=21_000_000, transcendentals=0),
    )(layer_input, up_cotangent, attn_values, resid_cotangent, feedback[0], start_seed)
    return (update.T, new_feedback[None])


def solution(mesh):
    in_specs = (
        P(("replica", "group"), None),
        P(("replica", "group"), None),
        P(("replica", "group"), None),
        P(("replica", "group"), None),
        P("replica", "group", None),
        P(),
    )
    out_specs = (P(None, "replica"), P("replica", "group", None))
    return jax.shard_map(
        on_device, mesh=mesh, in_specs=in_specs, out_specs=out_specs, check_vma=False
    )
```

```python
import jax
import jax.numpy as jnp
from jax import lax
from jax.experimental import pallas as pl
from jax.experimental.pallas import tpu as pltpu
from jax.sharding import PartitionSpec as P

RANK = 32
TOK = 768
D = 4096
FF = 1792
HD = 512
W = FF + HD
HALF = W // 2
ROWS = 256
SIDE = 4
GROUP = 16
REP = 8
BLEN = 1536
LEVELS = 32700.0
ORDER = (2, 1, 3, 0)
MESH = pl.DeviceIdType.MESH
F32 = jnp.float32
BF16 = jnp.bfloat16
OPP_A, OPP_B, PURE_B, PURE_A, DEP_A, DEP_B = range(6)
RIGHTWARD = (True, False, True, False, True, False)


def modulo(v):
    r = v - jnp.floor(v * (1.0 / 65521.0)) * 65521.0
    r = jnp.where(r < 0.0, r + 65521.0, r)
    return jnp.where(r >= 65521.0, r - 65521.0, r)


def factor_t(seed, first, count, layer):
    positions = lax.broadcasted_iota(jnp.int32, (RANK, count), 1) + first
    columns = lax.broadcasted_iota(jnp.int32, (RANK, count), 0)
    base = (seed % 65521) * 31 + layer * 4099 + 12345
    mixed = modulo((base + positions * 977 + columns * 7919).astype(F32)).astype(jnp.int32)
    folded = (mixed & 255) * (mixed >> 8)
    final = modulo((folded * 181 + mixed).astype(F32))
    return (final / 65521.0 - 0.5) * 3.4


def split3(v):
    hi = v.astype(BF16)
    rest = v - hi.astype(F32)
    mid = rest.astype(BF16)
    low = (rest - mid.astype(F32)).astype(BF16)
    return jnp.concatenate([hi, mid, low], axis=0)


def split2(v):
    hi = v.astype(BF16)
    return hi, (v - hi.astype(F32)).astype(BF16)


def fold3(v):
    return (v[64:96] + v[32:64]) + v[0:32]


def dot_nn(a, b):
    return lax.dot_general(a, b, (((1,), (0,)), ((), ())), preferred_element_type=F32)


def dot_nt(a, b):
    return lax.dot_general(a, b, (((1,), (1,)), ((), ())), preferred_element_type=F32)


def dot_tn(a, b):
    return lax.dot_general(a, b, (((0,), (0,)), ((), ())), preferred_element_type=F32)


def dot_nt_full(a, b):
    return lax.dot_general(
        a, b, (((1,), (1,)), ((), ())), precision=lax.Precision.HIGHEST, preferred_element_type=F32
    )


def peak8(v):
    return jnp.max(jnp.abs(v).reshape(v.shape[0] // 8, 8, v.shape[1]), axis=0)


def at(start, size, step):
    return pl.ds(pl.multiple_of(start, step), size)


def pieces3(v):
    hi = v.astype(BF16)
    rest = v - hi.astype(F32)
    mid = rest.astype(BF16)
    return hi, mid, (rest - mid.astype(F32)).astype(BF16)


def apply_factor(t_t, v):
    hi, mid, low = pieces3(t_t)
    left = jnp.concatenate([hi, hi, hi, mid, mid, low], axis=0)
    hi, mid, low = pieces3(v)
    return dot_tn(left, jnp.concatenate([hi, mid, low, hi, mid, hi], axis=0))


def eliminate(state, first, last):
    row = lax.broadcasted_iota(jnp.int32, (RANK, RANK), 0)
    lane = lax.broadcasted_iota(jnp.int32, (RANK, RANK), 1)

    def step(j, state):
        out = []
        for a, b in state:
            a_row = jnp.sum(jnp.where(row == j, a, 0.0), axis=0, keepdims=True)
            pivot = jnp.sum(jnp.where(lane[:1] == j, a_row, 0.0), axis=1, keepdims=True)
            a_col = jnp.sum(jnp.where(lane == j, a, 0.0), axis=1, keepdims=True)
            b_col = jnp.sum(jnp.where(lane == j, b, 0.0), axis=1, keepdims=True)
            factor = jnp.where(lane[:1] > j, a_row / pivot, 0.0)
            out.append((a - a_col * factor, b - b_col * factor))
        return tuple(out)

    return lax.fori_loop(first, last, step, state)


def identity():
    row = lax.broadcasted_iota(jnp.int32, (RANK, RANK), 0)
    lane = lax.broadcasted_iota(jnp.int32, (RANK, RANK), 1)
    return jnp.where(row == lane, 1.0, 0.0).astype(F32)


def scaled(state):
    eye = identity()
    return [b * (1.0 / jnp.sqrt(jnp.sum(a * eye, axis=0, keepdims=True))) for a, b in state]


def kernel(
    x_hbm, u_hbm, a_hbm, g_hbm, fb_hbm, seed_ref,
    fb, uout,
    xs, gs, ut, ustg, tmp, pdep, pown, tx, rx, q3,
    pt, pc, ps, py, pz, px, pall,
    bt, bc, bs, by, bz, bx, ball, bk4,
    load_x, load_g, load_u, load_fb,
    tx_sem, rx_sem, small_tx, small_rx,
):
    group = lax.axis_index("group")
    rep = lax.axis_index("replica")
    gx = group // SIDE
    gz = group % SIDE
    ry = rep // 2
    rc = rep % 2

    def member(dx, dz):
        return (gx + dx) % SIDE * SIDE + (gz + dz) % SIDE

    def replica(dy, dc):
        return (ry + dy) % SIDE * 2 + (rc + dc) % 2

    def load_step(k, j):
        df, ds = ORDER[j], ORDER[k]
        low = at(ROWS * member(df, ds), 128, 128)
        high = at(ROWS * member(ds, df) + 128, 128, 128)
        for src, dst, sem in ((x_hbm, xs, load_x), (g_hbm, gs, load_g)):
            for part, lanes in enumerate((low, high)):
                pltpu.make_async_copy(
                    src.at[:, lanes], dst.at[k, :, pl.ds(256 * j + 128 * part, 128)], sem.at[4 * k + j]
                ).start()

    load_a = pltpu.make_async_copy(u_hbm.at[:, pl.ds(0, HALF)], ustg, load_u.at[0])
    load_b = pltpu.make_async_copy(
        u_hbm.at[:, pl.ds(HALF, FF - HALF)], ustg.at[:, pl.ds(0, FF - HALF)], load_u.at[1]
    )
    load_c = pltpu.make_async_copy(a_hbm, ustg.at[:, pl.ds(FF - HALF, HD)], load_u.at[2])
    def load_rest():
        for k in range(SIDE):
            for j in range(SIDE):
                if k > 0 or j == SIDE - 1:
                    load_step(k, j)
        pltpu.make_async_copy(fb_hbm, fb, load_fb).start()

    loaded = set()

    def wait_step(k, j):
        if (k, j) in loaded:
            return
        loaded.add((k, j))
        for ref, sem in ((xs, load_x), (gs, load_g)):
            part = ref.at[k, :, pl.ds(256 * j, 256)]
            pltpu.make_async_copy(part, part, sem.at[4 * k + j]).wait()

    barrier = pltpu.get_barrier_semaphore()

    def greet(dy, dc, dx, dz):
        pl.semaphore_signal(
            barrier,
            inc=1,
            device_id={"replica": replica(dy, dc), "group": member(dx, dz)},
            device_id_type=MESH,
        )

    load_a.start()
    load_step(0, 0)
    greet(0, 1, 0, 0)
    for d in range(1, SIDE):
        greet(d, 0, 0, 0)
        greet(1, 0, 0, d)
        greet(SIDE - 1, 0, 0, d)
        greet(0, 0, d, 0)
    greet(0, 0, 0, 1)
    greet(0, 0, 0, SIDE - 1)

    def transpose_u(base, sizes):
        start = 0
        for size in sizes:
            ut[base + start : base + start + size, :] = ustg[:, start : start + size].T
            start += size

    A_TILES = ((0, HALF, xs),)
    B_TILES = ((HALF, FF - HALF, xs), (FF, HD, gs))

    def products(k, lanes, tiles):
        row = 0
        for start, size, source in tiles:
            yield row, size, dot_nn(ut[start : start + size, :], source[k, :, lanes])
            row += size

    def matmul(k, j, tiles, dst, base):
        peak = jnp.zeros((8, ROWS), F32)
        for row, size, value in products(k, slice(256 * j, 256 * j + 256), tiles):
            dst[base + row : base + row + size, :] = value
            peak = jnp.maximum(peak, peak8(value))
        return peak

    def matmul_pair(k, tiles, dst_1, base_1, dst_2, base_2):
        peak = jnp.zeros((8, 2 * ROWS), F32)
        for row, size, value in products(k, slice(256, 768), tiles):
            dst_1[base_1 + row : base_1 + row + size, :] = value[:, :ROWS]
            dst_2[base_2 + row : base_2 + row + size, :] = value[:, ROWS:]
            peak = jnp.maximum(peak, peak8(value))
        return peak[:, :ROWS], peak[:, ROWS:]

    def quantise(src, base, m, slot):
        peak = jnp.maximum(jnp.max(m, axis=0, keepdims=True), 1e-30)
        power = jnp.ceil(jnp.log2(peak))
        scale = jnp.exp2(-power) * LEVELS

        @pl.loop(0, HALF // 64)
        def _(t):
            v = src[at(base + t * 64, 64, 64), :] * scale
            tx[slot, at(t * 64, 64, 64), :] = jnp.round(v).astype(jnp.int32).astype(jnp.int16)

        tx[slot, HALF : HALF + 16, :] = jnp.broadcast_to(power, (16, ROWS)).astype(jnp.int32).astype(jnp.int16)

    def copy_of(slot, mid, kind, stage, h):
        lanes = pl.ds(128 * h, 128)
        along_x = (h == 0) == (stage == 0)
        step = 1 if RIGHTWARD[kind] else SIDE - 1
        peer = member(step, 0) if along_x else member(0, step)
        return pltpu.make_async_remote_copy(
            src_ref=tx.at[slot, :, lanes],
            dst_ref=rx.at[mid, :, lanes],
            send_sem=tx_sem.at[mid, h],
            recv_sem=rx_sem.at[mid, h],
            device_id={"group": peer},
            device_id_type=MESH,
        )

    def slot_of(mid):
        chunk, kind = divmod(mid, 6)
        if chunk == 4:
            return 8 + kind
        return kind + (6 if chunk % 2 and kind < 2 else 0)

    def copies(mid):
        chunk, kind = divmod(mid, 6)
        return [copy_of(slot_of(mid), mid, kind, chunk // 4, h) for h in range(2)]

    pending = {}

    def send(mid, src, base, m, held=()):
        slot = slot_of(mid)
        if slot in pending:
            for c in copies(pending[slot]):
                c.wait_send()
        quantise(src, base, m, slot)
        for h, c in enumerate(copies(mid)):
            if h not in held:
                c.start()
        pending[slot] = mid

    def release(mid, h):
        copies(mid)[h].start()

    def scale_of(mid):
        power = rx[mid, HALF : HALF + 16, :].astype(jnp.int32).astype(F32)[:8]
        return jnp.exp2(power) * (1.0 / LEVELS)

    def combine(acc, base, mids):
        for mid in mids:
            for c in copies(mid):
                c.wait_recv()
        scales = [scale_of(mid) for mid in mids]

        def tile(t, m):
            v = acc[at(base + t * 64, 64, 64), :].reshape(8, 8, ROWS)
            for mid, scale in zip(mids, scales):
                got = rx[mid, at(t * 64, 64, 64), :].astype(jnp.int32).astype(F32).reshape(8, 8, ROWS)
                v = v + got * scale[None]
            acc[at(base + t * 64, 64, 64), :] = v.reshape(64, ROWS)
            return jnp.maximum(m, jnp.max(jnp.abs(v), axis=0))

        return lax.fori_loop(0, HALF // 64, tile, jnp.zeros((8, ROWS), F32))

    def opposite_a(k, held=()):
        wait_step(k, 0)
        m = matmul(k, 0, A_TILES, tmp, 0)
        send(6 * k + OPP_A, tmp, 0, m, held)

    def opposite_b(k):
        wait_step(k, 0)
        m = matmul(k, 0, B_TILES, tmp, 0)
        send(6 * k + OPP_B, tmp, 0, m)

    def pure_b(k, held=()):
        wait_step(k, 1)
        wait_step(k, 2)
        m, _ = matmul_pair(k, B_TILES, tmp, 0, pdep, HALF)
        send(6 * k + PURE_B, tmp, 0, m, held)

    def pure_a(k):
        wait_step(k, 1)
        wait_step(k, 2)
        _, m = matmul_pair(k, A_TILES, pdep, 0, tmp, 0)
        send(6 * k + PURE_A, tmp, 0, m)

    def own(k):
        wait_step(k, 3)
        matmul(k, 3, A_TILES, pown, 0)
        matmul(k, 3, B_TILES, pown, HALF)

    def dependent_a(k):
        m = combine(pdep, 0, [6 * k + OPP_A])
        send(6 * k + DEP_A, pdep, 0, m)

    def dependent_b(k):
        m = combine(pdep, HALF, [6 * k + OPP_B])
        send(6 * k + DEP_B, pdep, HALF, m)

    def complete_a(k):
        more = {0: [], 1: [24 + OPP_A], 2: []}[k]
        m = combine(pown, 0, [6 * k + DEP_A, 6 * k + PURE_A] + more)
        send(24 + (OPP_A, DEP_A, PURE_A)[k], pown, 0, m)

    def complete_b(k):
        more = {0: [], 1: [], 2: [24 + OPP_B]}[k]
        m = combine(pown, HALF, [6 * k + PURE_B, 6 * k + DEP_B] + more)
        send(24 + (OPP_B, PURE_B, DEP_B)[k], pown, HALF, m)

    def finish(base, mids, with_own):
        for mid in mids:
            for c in copies(mid):
                c.wait_recv()
        scales = [scale_of(mid) for mid in mids]
        for t in range(HALF // 128):
            rows = slice(128 * t, 128 * t + 128)
            v = pown[base + 128 * t : base + 128 * t + 128, :].reshape(16, 8, ROWS) if with_own else None
            for mid, scale in zip(mids, scales):
                got = rx[mid, rows, :].astype(jnp.int32).astype(F32).reshape(16, 8, ROWS) * scale[None]
                v = got if v is None else v + got
            columns = slice(base + 128 * t, base + 128 * t + 128)
            fb[:, columns] += v.reshape(128, ROWS).T * (1.0 / GROUP)

    def post(src, dst, which, dy, dc, dx, dz):
        pltpu.make_async_remote_copy(
            src_ref=src,
            dst_ref=dst,
            send_sem=small_tx.at[which],
            recv_sem=small_rx.at[which],
            device_id={"replica": replica(dy, dc), "group": member(dx, dz)},
            device_id_type=MESH,
        ).start()

    def await_bytes(ref, sem):
        pltpu.make_async_copy(ref, ref, sem).wait()

    def all_reduce(src, core, total, chips, zs, xs_, result, first):
        length = src.shape[1]
        quarter = length // SIDE
        core_rows = at(rc * 32, 32, 32)
        my_rows = at(rc * 32 + ry * 8, 8, 8)

        def start():
            post(src.at[at((1 - rc) * 32, 32, 32), :], core, first, 0, 1, 0, 0)

        def along_y():
            await_bytes(core, small_rx.at[first])
            total[...] = src[core_rows, :] + core[...]
            for d in range(1, SIDE):
                post(total.at[at((ry + d) % SIDE * 8, 8, 8), :], chips.at[d - 1], first + 1, d, 0, 0, 0)

        def along_z():
            await_bytes(chips.at[pl.ds(0, 3)], small_rx.at[first + 1])
            chips[3] = (total[at(ry * 8, 8, 8), :] + chips[0]) + (chips[1] + chips[2])
            for d in range(SIDE):
                lanes = at((gz + d) % SIDE * quarter, quarter, 128)
                post(chips.at[3, :, lanes], zs.at[d], first + 2, 1, 0, 0, d)

        def along_x():
            await_bytes(zs.at[pl.ds(0, 4)], small_rx.at[first + 2])
            zs[4] = (zs[0] + zs[1]) + (zs[2] + zs[3])
            for d in range(1, SIDE):
                post(zs.at[4], xs_.at[gx], first + 3, 0, 0, d, 0)
            xs_[gx] = zs[4]

        def back_z():
            await_bytes(xs_.at[pl.ds(0, 3)], small_rx.at[first + 3])
            xs_[4] = (xs_[0] + xs_[1]) + (xs_[2] + xs_[3])
            rows = at(rc * 32 + (ry + SIDE - 1) % SIDE * 8, 8, 8)
            for d in range(SIDE):
                post(
                    xs_.at[4], result.at[rows, at(gz * quarter, quarter, 128)], first + 4, SIDE - 1, 0, 0, d
                )

        def back_y():
            await_bytes(result.at[pl.ds(0, 8), :], small_rx.at[first + 4])
            for d in range(1, SIDE):
                post(result.at[my_rows, :], result.at[my_rows, :], first + 5, d, 0, 0, 0)

        def back_core():
            await_bytes(result.at[pl.ds(0, 24), :], small_rx.at[first + 5])
            post(result.at[core_rows, :], result.at[core_rows, :], first + 6, 0, 1, 0, 0)

        def done():
            await_bytes(result.at[pl.ds(0, 32), :], small_rx.at[first + 6])

        def sent():
            await_bytes(result.at[pl.ds(0, 32), :], small_tx.at[first])
            await_bytes(result.at[pl.ds(0, 24), :], small_tx.at[first + 1])
            await_bytes(result.at[pl.ds(0, 8), :], small_tx.at[first + 2])
            await_bytes(xs_.at[pl.ds(0, 3)], small_tx.at[first + 3])
            await_bytes(result.at[pl.ds(0, 8), :], small_tx.at[first + 4])
            await_bytes(result.at[pl.ds(0, 24), :], small_tx.at[first + 5])
            await_bytes(result.at[pl.ds(0, 32), :], small_tx.at[first + 6])

        return start, along_y, along_z, along_x, back_z, back_y, back_core, done, sent

    def lanes_of(k, j):
        df, ds = ORDER[j], ORDER[k]
        return at(ROWS * member(df, ds), 128, 128), at(ROWS * member(ds, df) + 128, 128, 128)

    def make_factors():
        seed = seed_ref[0]
        for t in range(9):
            layer = t // 7
            q = factor_t(seed, 256 * (t - 7 * layer), 256, layer)
            q3[:, 256 * t : 256 * t + 256] = split3(q)

    def project():
        w_l = split3(fold3(dot_nn(q3[:, :FF], ut[:FF, :])))
        w_r = split3(fold3(dot_nn(q3[:, FF:], ut[FF:, :])))
        for k in range(SIDE):
            p_l = fold3(dot_nn(w_l, xs[k])) * (1.0 / 128)
            p_r = fold3(dot_nn(w_r, gs[k])) * (1.0 / 128)
            for j in range(SIDE):
                for part, lanes in enumerate(lanes_of(k, j)):
                    here = slice(256 * j + 128 * part, 256 * j + 128 * part + 128)
                    pt[:RANK, lanes] = p_l[:, here]
                    pt[RANK:, lanes] = p_r[:, here]

        mine = at(ROWS * group, ROWS, 128)
        for rows, columns in ((slice(0, RANK), slice(0, FF)), (slice(RANK, 64), slice(FF, W))):
            hi, low = split2(fb[:, columns])
            term = fold3(dot_nt(q3[:, columns], hi)) + fold3(dot_nt(q3[:, columns], low))
            pt[rows, mine] += term * (1.0 / 8)

    def back_project():
        y_l = jnp.zeros((96, TOK), F32)
        y_r = jnp.zeros((96, TOK), F32)
        for k in range(SIDE):
            parts = []
            for j in range(SIDE):
                for lanes in lanes_of(k, j):
                    parts.append(pall[:, lanes])
            p = jnp.concatenate(parts, axis=1)
            y_l = y_l + dot_nt(split3(p[:RANK]), xs[k])
            y_r = y_r + dot_nt(split3(p[RANK:]), gs[k])
        y_l = split3(fold3(y_l) * (1.0 / 128))
        y_r = split3(fold3(y_r) * (1.0 / 128))
        p = pall[:, at(ROWS * group, ROWS, 128)] * (1.0 / 8)
        p_l, p_r = split3(p[:RANK]), split3(p[RANK:])

        def piece(y, p3, columns):
            hi, low = split2(fb[:, columns])
            return fold3(dot_nt(y, ut[columns, :])) + (fold3(dot_nn(p3, hi)) + fold3(dot_nn(p3, low)))

        bt[:RANK, :HALF] = piece(y_l, p_l, slice(0, HALF))
        bt[RANK:, 0:640] = piece(y_l, p_l, slice(HALF, FF))
        bt[RANK:, 640:HALF] = piece(y_r, p_r, slice(FF, W))
        bt[:, HALF:] = jnp.zeros((64, BLEN - HALF), F32)

    def grams():
        eye = identity()
        return tuple(
            (dot_nt_full(pall[rows, :], pall[rows, :]), eye) for rows in (slice(0, RANK), slice(RANK, 64))
        )

    def quad(v, last):
        hi, low = split2(v)
        return jnp.concatenate([hi, hi, low, low] if last else [hi, low, hi, low], axis=0)

    def bases(t_l, t_r, lanes):
        return jnp.concatenate(
            [
                quad(apply_factor(t_l, pall[:RANK, lanes]), True),
                quad(apply_factor(t_r, pall[RANK:, lanes]), True),
            ],
            axis=0,
        )

    def decompress(t_l, t_r):
        mine = bases(t_l, t_r, at(ROWS * group, ROWS, 128)).T
        pieces = (
            (t_l, slice(0, RANK), 0, HALF, 0),
            (t_l, slice(RANK, 64), 0, 640, HALF),
            (t_r, slice(RANK, 64), 640, HALF, HALF),
        )
        for t, rows, lo, hi, base in pieces:
            b4 = quad(apply_factor(t, ball[rows, lo:hi]), False)
            none = jnp.zeros_like(b4)
            left = base + lo < FF
            both = jnp.concatenate([b4, none] if left else [none, b4], axis=0)
            fb[:, base + lo : base + hi] -= dot_nn(mine, both)
            bk4[base + lo : base + hi, :] = both.T

    def decompress_update(t_l, t_r):
        width = W // REP
        chosen = bk4[at(rep * width, width, 16), :]
        for t in range(4):
            lanes = slice(1024 * t, 1024 * t + 1024)
            uout[:, lanes] = dot_nn(chosen, bases(t_l, t_r, lanes)).astype(BF16)

    p_steps = all_reduce(pt, pc, ps, py, pz, px, pall, 0)
    b_steps = all_reduce(bt, bc, bs, by, bz, bx, ball, 7)

    load_step(0, 1)
    load_step(0, 2)
    make_factors()
    load_a.wait()
    transpose_u(0, (384, 384, 384))
    load_b.start()
    load_c.start()
    pl.semaphore_wait(barrier, 15)
    opposite_a(0)
    load_b.wait()
    load_c.wait()
    transpose_u(HALF, (256, 384, 256, 256))
    load_rest()
    opposite_b(0)
    pure_b(0)
    pure_a(0)
    opposite_b(1)
    for k in range(SIDE):
        for j in range(SIDE):
            wait_step(k, j)
    pltpu.make_async_copy(fb_hbm, fb, load_fb).wait()
    project()
    p_steps[0]()
    opposite_a(1)
    dependent_a(0)
    p_steps[1]()
    dependent_b(0)
    own(0)
    pure_b(1)
    pure_a(1)
    p_steps[2]()
    p_steps[3]()
    dependent_a(1)
    dependent_b(1)
    complete_a(0)
    complete_b(0)
    opposite_a(2)
    opposite_b(2)
    own(1)
    p_steps[4]()
    pure_b(2)
    pure_a(2)
    p_steps[5]()
    dependent_a(2)
    dependent_b(2)
    p_steps[6]()
    complete_a(1)
    complete_b(1)
    p_steps[7]()
    back_project()
    b_steps[0]()
    opposite_b(3)
    opposite_a(3, held=(0,))
    b_steps[1]()
    own(2)
    pure_a(3)
    pure_b(3, held=(0,))
    state = eliminate(grams(), 0, 8)
    b_steps[2]()
    state = eliminate(state, 8, 20)
    b_steps[3]()
    release(18 + OPP_A, 0)
    release(18 + PURE_B, 0)
    complete_b(2)
    complete_a(2)
    state = eliminate(state, 20, RANK)
    t_l, t_r = scaled(state)
    b_steps[4]()
    own(3)
    dependent_b(3)
    b_steps[5]()
    dependent_a(3)
    b_steps[6]()
    finish(0, [18 + PURE_A, 24 + DEP_A, 24 + PURE_A], True)
    finish(HALF, [18 + PURE_B, 24 + PURE_B, 24 + DEP_B], True)
    b_steps[7]()
    decompress(t_l, t_r)
    decompress_update(t_l, t_r)
    finish(HALF, [18 + DEP_B], False)
    finish(0, [18 + DEP_A], False)

    for slot in pending:
        for c in copies(pending[slot]):
            c.wait_send()
    p_steps[8]()
    b_steps[8]()


def small_buffers(length):
    quarter = length // SIDE
    shapes = (
        (64, length), (32, length), (32, length), (4, 8, length), (5, 8, quarter), (5, 8, quarter), (64, length)
    )
    return [pltpu.VMEM(shape, F32) for shape in shapes]


def on_device(layer_input, up_cotangent, attn_values, resid_cotangent, feedback, start_seed):
    hbm = pl.BlockSpec(memory_space=pl.ANY)
    vmem = pl.BlockSpec(memory_space=pltpu.VMEM)
    dma = pltpu.SemaphoreType.DMA
    new_feedback, update = pl.pallas_call(
        kernel,
        out_shape=(
            pltpu.VMEM((ROWS, W), F32),
            pltpu.VMEM((W // REP, D), BF16),
        ),
        in_specs=[hbm] * 5 + [pl.BlockSpec(memory_space=pltpu.SMEM)],
        out_specs=(vmem, vmem),
        scratch_shapes=[
            pltpu.VMEM((SIDE, TOK, SIDE * ROWS), BF16),
            pltpu.VMEM((SIDE, TOK, SIDE * ROWS), BF16),
            pltpu.VMEM((W, TOK), BF16),
            pltpu.VMEM((TOK, HALF), BF16),
            pltpu.VMEM((HALF, ROWS), F32),
            pltpu.VMEM((W, ROWS), F32),
            pltpu.VMEM((W, ROWS), F32),
            pltpu.VMEM((14, HALF + 16, ROWS), jnp.int16),
            pltpu.VMEM((30, HALF + 16, ROWS), jnp.int16),
            pltpu.VMEM((96, W), BF16),
            *small_buffers(D),
            *small_buffers(BLEN),
            pltpu.VMEM((W, 256), BF16),
            dma((GROUP,)),
            dma((GROUP,)),
            dma((3,)),
            dma,
            dma((30, 2)),
            dma((30, 2)),
            dma((14,)),
            dma((14,)),
        ],
        compiler_params=pltpu.CompilerParams(
            collective_id=0, has_side_effects=True, vmem_limit_bytes=58 * 1024 * 1024
        ),
        cost_estimate=pl.CostEstimate(flops=2 * TOK * D * W, bytes_accessed=21_000_000, transcendentals=0),
    )(layer_input, up_cotangent, attn_values, resid_cotangent, feedback[0], start_seed)
    return (update.T, new_feedback[None])


def solution(mesh):
    in_specs = (
        P(("replica", "group"), None),
        P(("replica", "group"), None),
        P(("replica", "group"), None),
        P(("replica", "group"), None),
        P("replica", "group", None),
        P(),
    )
    out_specs = (P(None, "replica"), P("replica", "group", None))
    return jax.shard_map(
        on_device, mesh=mesh, in_specs=in_specs, out_specs=out_specs, check_vma=False
    )
```
